32 devices in a mesh: groups: 2 (over y), seq: 4 (over x, core), heads: 4 (over z).
Axes of the slice: x: 2, y: 2, z: 4, core: 2. Of those that a mesh axis runs over, the one named last changes fastest.
Arguments:
- prompt_states: bfloat16 [6144, 7168], P(('groups', 'seq'), 'heads'), parts along dimension 0, may hold values from -6 to 6
- new_states: bfloat16 [512, 7168], P(('groups', 'seq'), 'heads'), parts along dimension 0, may hold values from -6 to 6
- prompt_lengths: int32 [8, 16], P('groups'), parts along dimension 0, may hold values from 1 to 128, 768 in all within a row
- routing: int32 [8, 16], P('groups'), parts along dimension 0, may hold values from 0 to 15, each once within a row
- row_request: int32 [512], P(('groups', 'seq')), parts along dimension 0, may hold values from 0 to 15
- queries: bfloat16 [512, 128, 192], P(('groups', 'seq'), 'heads'), parts along dimension 0, may hold values from -68 to 68
- gain_kv: float32 [512], replicated, may hold values from 0.5 to 1.5
- down_kv: bfloat16 [7168, 576], P('heads'), may hold values from -0.0625 to 0.0625
- absorb_k: bfloat16 [128, 128, 512], P('heads'), may hold values from -0.25 to 0.25
- absorb_v: bfloat16 [128, 512, 128], P('heads'), may hold values from -0.25 to 0.25
- out_proj: bfloat16 [16384, 7168], P('heads', 'seq'), may hold values from -0.1875 to 0.1875
Outputs:
- attended: bfloat16 [512, 7168], P(('groups', 'heads'), 'seq'), parts along dimension 0
The draws below stay inside these ranges and needn't reach their ends.
There are 2 independent parts, one for each index of `groups`. The reference program is written for one: setup_inputs(seed, part) draws one part's arguments, and reference() takes and returns one part's arrays. A program takes and returns all parts, laid end to end along the dimension named above; an argument that names none is the same for every part. Nothing has to cross between parts.
Inputs may be any that keep to these rules, and one draw needn't show every extreme that they name: `prompt_lengths`: each row lists the 16 prompt lengths of one prefill index, packed in this order in its 768 rows; each row sums to 768 and reaches 128. `routing`: each row is a permutation of 0 to 15.
All inputs are finite; a program needn't handle non-finite values.
Results may differ from the reference program's by a relative error of at most 0.012.
The reference program's roundings to bfloat16 on the way count: a program that leaves them out, or rounds other values in their place, can miss the bound.
Values may be sent and summed in bfloat16 or wider, within the bound.
A program may use at most 128 MiB of HBM per device.

```python
import math
import jax
import jax.numpy as jnp
import numpy as np
from jax import lax

D = 7168
H = 128
KVL = 512
ROPE = 64
NOPE = 128
VHEAD = 128
REQ_DEV = 16
MAXLEN = 128
OWNERS = 4
PER = 4
PR_DEV = 768
DEC_DEV = 64
PROMPT_ROWS = 3072
DEC_ROWS = 256


def draw_queries(key, part):
    key = jax.random.fold_in(key, 7)
    array_shape = (DEC_ROWS, H, NOPE + ROPE)
    values = jnp.clip(jax.random.normal(key, array_shape, jnp.float32), -4.0, 4.0)
    return values.astype(jnp.bfloat16)


def plant(array, rng, least, largest):
    extent = array.shape
    spot = [jax.random.randint(jax.random.fold_in(rng, axis), (), 0, extent[axis]) for axis in range(len(extent))]
    array = array.at[tuple(spot)].set(least)
    longest = extent.index(max(extent))
    spot[longest] = (spot[longest] + 1) % extent[longest]
    return array.at[tuple(spot)].set(largest)


def level_of(key, shape, split, low, top_value):
    factor_of = 1.0
    for dim, shards_of in split:
        steps = jax.random.uniform(jax.random.fold_in(jax.random.fold_in(key, 6), dim), (shards_of,), jnp.float32, low / len(split), top_value / len(split))
        factor_of = factor_of * jnp.repeat(jnp.exp(steps), shape[dim] // shards_of).reshape((-1,) + (1,) * (len(shape) - 1 - dim))
    return factor_of


def profile(number_of, total, reach, lean):
    weights = [(1 << 20) // math.isqrt(grade ** lean) + 1 for grade in range(2, number_of + 1)]
    surplus, holding = total - reach - (number_of - 1), [1] * (number_of - 1)
    while surplus > 0:
        candidates = [i for i in range(number_of - 1) if holding[i] < reach]
        pool, budget = sum([weights[i] for i in candidates]), surplus
        for i in candidates:
            extra = min(reach - holding[i], max(1, budget * weights[i] // pool), surplus)
            holding[i] = holding[i] + extra
            surplus = surplus - extra
    return np.array([reach] + holding)


def uneven(key, count, total, reach, slope):
    if count == 2:
        one = jax.random.randint(key, (), max(1, total - reach), min(reach, total - 1) + 1)
        return jnp.stack([one, total - one])
    sizes = jnp.asarray(profile(count, total, reach, slope), jnp.int32)
    twos = (count - 1) // 2
    source_of, taker = sizes[1:1 + 2 * twos:2], sizes[2:2 + 2 * twos:2]
    room = jnp.minimum(source_of - 1, reach - taker)
    moved = jax.random.randint(jax.random.fold_in(key, 1), (twos,), 0, 1 << 20) % (room + 1)
    sizes = sizes.at[1:1 + 2 * twos:2].set(source_of - moved).at[2:2 + 2 * twos:2].set(taker + moved)
    return sizes[jax.random.permutation(jax.random.fold_in(key, 2), count)]


def centred(rng, shape, scale, bound, cuts=(), held_as=jnp.bfloat16):
    result = jax.random.normal(rng, shape, jnp.float32) * scale
    if len(cuts) > 0:
        result = level_of(rng, shape, cuts, -0.22, 0.18) * result
    return jnp.clip(result, min=-bound, max=bound).astype(held_as)


def setup_inputs(seed: int = 0, part: int = 0) -> dict:
    splits = jax.random.split(jax.random.key(seed), 12)
    own_keys = jax.random.split(jax.random.fold_in(splits[11], part), 12)
    return {
        "prompt_states": centred(own_keys[0], (PROMPT_ROWS, D), 1.0, 6.0, ((0, 4), (1, 4))),
        "new_states": centred(own_keys[1], (DEC_ROWS, D), 1.0, 6.0, ((0, 4), (1, 4))),
        "prompt_lengths": jax.vmap(lambda own: uneven(own, REQ_DEV, PR_DEV, MAXLEN, 2))(jax.random.split(own_keys[2], OWNERS)).reshape((OWNERS, REQ_DEV)).astype(jnp.int32),
        "routing": jax.vmap(lambda own: jax.random.permutation(own, REQ_DEV))(jax.random.split(own_keys[3], OWNERS)).reshape((OWNERS, REQ_DEV)).astype(jnp.int32),
        "row_request": plant(jax.random.randint(own_keys[4], (DEC_ROWS,), 0, REQ_DEV), jax.random.fold_in(own_keys[4], 1), 0, REQ_DEV - 1).astype(jnp.int32),
        "queries": draw_queries(jax.random.fold_in(jax.random.fold_in(splits[11], part), 71), part),
        "gain_kv": jnp.clip(1.0 + 0.1 * jax.random.normal(splits[6], (KVL,), jnp.float32), 0.5, 1.5),
        "down_kv": centred(splits[7], (D, KVL + ROPE), D ** -0.5, 0.0625, ((0, 4),)),
        "absorb_k": centred(splits[8], (H, NOPE, KVL), KVL ** -0.5, 0.25, ((0, 4),)),
        "absorb_v": centred(splits[9], (H, KVL, VHEAD), KVL ** -0.5, 0.25, ((0, 4),)),
        "out_proj": centred(splits[10], (H * VHEAD, D), (H * VHEAD // 16) ** -0.5, 0.1875, ((0, 4), (1, 4))),
    }


def rotate(part_e, positions):
    half = ROPE // 2
    order = jnp.arange(half, dtype=jnp.float32)
    freq = 10000.0 ** (-2.0 * order / ROPE)
    angle = positions.astype(jnp.float32)[:, None] * freq[None, :]
    cosine = jnp.cos(angle)
    sine = jnp.sin(angle)
    first_half = part_e[:, :half]
    second_half = part_e[:, half:]
    return jnp.concatenate([first_half * cosine - second_half * sine, first_half * sine + second_half * cosine], axis=1)

def finish_latent(projected, gain_kv, positions):
    content = projected[:, :KVL]
    inverse = lax.rsqrt(lax.optimization_barrier(jnp.mean(content * content, axis=1, keepdims=True)) + 1e-06)
    content = content * inverse * gain_kv[None, :]
    return jnp.concatenate([content, rotate(projected[:, KVL:], positions)], axis=1).astype(jnp.bfloat16)

def layout(prompt_lengths, routing, row_request):
    starts = jnp.cumsum(prompt_lengths, axis=1) - prompt_lengths
    finishes = starts + prompt_lengths
    row_ids = jnp.arange(PR_DEV, dtype=jnp.int32)
    holder = lax.optimization_barrier(jnp.sum((row_ids[None, :, None] >= finishes[:, None, :]).astype(jnp.int32), axis=2))
    row_start = jnp.take_along_axis(starts, holder, axis=1)
    prompt_pos = (row_ids[None, :] - row_start).reshape(-1)
    slot_ids = jnp.arange(REQ_DEV, dtype=jnp.int32)
    source = slot_ids // PER
    owners = jnp.arange(OWNERS, dtype=jnp.int32)
    column = owners[:, None] * PER + (slot_ids % PER)[None, :]
    slot_req = routing[source[None, :], column]
    slot_len = prompt_lengths[source[None, :], slot_req]
    slot_first = source[None, :] * PR_DEV + starts[source[None, :], slot_req]
    requests = row_request.reshape(OWNERS, DEC_DEV)
    same_slot = requests[:, :, None] == requests[:, None, :]
    before = jnp.arange(DEC_DEV)[:, None] > jnp.arange(DEC_DEV)[None, :]
    earlier = lax.optimization_barrier(jnp.sum((same_slot & before[None, :, :]).astype(jnp.int32), axis=2))
    new_pos = (jnp.take_along_axis(slot_len, requests, axis=1) + earlier).reshape(-1)
    return (prompt_pos, slot_len, slot_first, new_pos)

def reference(prompt_states, new_states, prompt_lengths, routing, row_request, queries, gain_kv, down_kv, absorb_k, absorb_v, out_proj):
    prompt_pos, slot_len, slot_first, new_pos = layout(prompt_lengths, routing, row_request)
    prompt_lat = finish_latent(jnp.dot(prompt_states, down_kv, preferred_element_type=jnp.float32), gain_kv, prompt_pos)
    new_lat = finish_latent(jnp.dot(new_states, down_kv, preferred_element_type=jnp.float32), gain_kv, new_pos)
    offsets = jnp.arange(MAXLEN, dtype=jnp.int32)
    token_ids = jnp.arange(DEC_DEV, dtype=jnp.int32)
    softmax_scale = 1.0 / math.sqrt(NOPE + ROPE)

    def one_owner(owner):
        own_lengths = slot_len[owner]
        first_rows = slot_first[owner]
        source_rows = jnp.clip(first_rows[:, None] + offsets[None, :], 0, PROMPT_ROWS - 1)
        usable = offsets[None, :] < own_lengths[:, None]
        kv_cache = jnp.where(usable[:, :, None], prompt_lat[source_rows], 0.0)
        start = owner * DEC_DEV
        requests = lax.dynamic_slice_in_dim(row_request, start, DEC_DEV)
        query_own = lax.dynamic_slice_in_dim(queries, start, DEC_DEV)
        new_own = lax.dynamic_slice_in_dim(new_lat, start, DEC_DEV)
        query_latent = jnp.einsum('thn,hnc->thc', query_own[:, :, :NOPE].astype(jnp.float32), absorb_k.astype(jnp.float32)).astype(jnp.bfloat16)
        query_full = jnp.concatenate([query_latent, query_own[:, :, NOPE:]], axis=2).astype(jnp.float32)
        row_cache = kv_cache[requests].astype(jnp.float32)
        row_len = own_lengths[requests]
        score_cache = jnp.einsum('thc,tpc->thp', query_full, row_cache) * softmax_scale
        score_new = jnp.einsum('thc,uc->thu', query_full, new_own.astype(jnp.float32)) * softmax_scale
        ok_cache = (offsets[None, :] < row_len[:, None])[:, None, :]
        ok_new = ((requests[:, None] == requests[None, :]) & (token_ids[None, :] <= token_ids[:, None]))[:, None, :]
        peak_score = jnp.maximum(lax.optimization_barrier(jnp.max(jnp.where(ok_cache, score_cache, -jnp.inf), axis=2)), lax.optimization_barrier(jnp.max(jnp.where(ok_new, score_new, -jnp.inf), axis=2)))
        exp_cache = jnp.where(ok_cache, jnp.exp(score_cache - peak_score[:, :, None]), 0.0)
        exp_new = jnp.where(ok_new, jnp.exp(score_new - peak_score[:, :, None]), 0.0)
        denominator = lax.optimization_barrier(jnp.sum(exp_cache, axis=2)) + lax.optimization_barrier(jnp.sum(exp_new, axis=2))
        weight_cache = (exp_cache / denominator[:, :, None]).astype(jnp.bfloat16)
        weight_new = (exp_new / denominator[:, :, None]).astype(jnp.bfloat16)
        latent_out = jnp.einsum('thp,tpc->thc', weight_cache.astype(jnp.float32), row_cache[:, :, :KVL])
        latent_out = latent_out + jnp.einsum('thu,uc->thc', weight_new.astype(jnp.float32), new_own[:, :KVL].astype(jnp.float32))
        latent_out = latent_out.astype(jnp.bfloat16)
        head_out = jnp.einsum('thc,hcv->thv', latent_out.astype(jnp.float32), absorb_v.astype(jnp.float32)).astype(jnp.bfloat16)
        return head_out.reshape(DEC_DEV, H * VHEAD)
    head_out = lax.map(one_owner, jnp.arange(OWNERS, dtype=jnp.int32)).reshape(DEC_ROWS, H * VHEAD)
    return jnp.dot(head_out, out_proj, preferred_element_type=jnp.float32).astype(jnp.bfloat16)
```

```python
import functools
import math

import jax
import jax.numpy as jnp
from jax import lax
from jax.experimental import pallas as pl
from jax.experimental.pallas import tpu as pltpu
from jax.sharding import PartitionSpec as P

KVL = 512
ROPE = 64
NOPE = 128
MAXLEN = 128


MESH = pl.DeviceIdType.MESH


def rotation_tables(positions):
    half = ROPE // 2
    order = jnp.arange(half, dtype=jnp.float32)
    freq = 10000.0 ** (-2.0 * order / ROPE)
    angle = positions.astype(jnp.float32)[:, None] * freq[None, :]
    cosine = jnp.cos(angle)
    sine = jnp.sin(angle)
    return (
        jnp.concatenate([cosine, cosine], axis=1),
        jnp.concatenate([-sine, sine], axis=1),
    )


def latent_kernel(
    heads,
    seq,
    x_ref,
    n_ref,
    w_ref,
    gain_ref,
    cos_ref,
    sin_ref,
    cache_ref,
    new_ref,
    new_part,
    out_buf,
    from_left,
    from_right,
    rs_send,
    rs_left,
    rs_right,
    ag_send,
    ag_recv,
    x_send,
    x_recv,
    sib_send,
    sib_recv,
):
    h = lax.axis_index("heads")
    s = lax.axis_index("seq")
    sibling = s + 1 - 2 * lax.rem(s, 2)
    cp = x_ref.shape[0] // heads
    pn = n_ref.shape[0] // heads
    others = seq // 2 - 1

    barrier = pltpu.get_barrier_semaphore()

    def greet(where):
        pl.semaphore_signal(barrier, inc=1, device_id=where, device_id_type=MESH)

    @pl.when(h > 0)
    def _():
        greet({"heads": h - 1})

    @pl.when(h < heads - 1)
    def _():
        greet({"heads": h + 1})

    greet({"seq": sibling})
    for j in range(1, others + 1):
        greet({"seq": lax.rem(s + 2 * j, seq)})
    pl.semaphore_wait(
        barrier,
        1 + others + jnp.where(h > 0, 1, 0) + jnp.where(h < heads - 1, 1, 0),
    )

    new_part[...] = jnp.dot(n_ref[...], w_ref[...], preferred_element_type=jnp.float32)

    def partial(c):
        rows = x_ref[pl.ds(pl.multiple_of(c * cp, 16), cp), :]
        top = jnp.dot(rows, w_ref[...], preferred_element_type=jnp.float32)
        return jnp.concatenate([top, new_part[pl.ds(pl.multiple_of(c * pn, 16), pn), :]], axis=0)

    def send_right(c):
        return pltpu.make_async_remote_copy(
            src_ref=out_buf.at[c],
            dst_ref=from_left.at[c],
            send_sem=rs_send.at[c],
            recv_sem=rs_left.at[c],
            device_id={"heads": h + 1},
            device_id_type=MESH,
        )

    def send_left(c):
        return pltpu.make_async_remote_copy(
            src_ref=out_buf.at[c],
            dst_ref=from_right.at[c],
            send_sem=rs_send.at[c],
            recv_sem=rs_right.at[c],
            device_id={"heads": h - 1},
            device_id_type=MESH,
        )

    for i in range(heads - 1):
        right, left = heads - 1 - i, i

        @pl.when(h < right)
        def _():
            @pl.when(h == 0)
            def _():
                out_buf[right] = partial(right).astype(jnp.bfloat16)

            @pl.when(h > 0)
            def _():
                mine = partial(right)
                send_right(right).wait_recv()
                out_buf[right] = (mine + from_left[right].astype(jnp.float32)).astype(jnp.bfloat16)

            send_right(right).start()

        @pl.when(h > left)
        def _():
            @pl.when(h == heads - 1)
            def _():
                out_buf[left] = partial(left).astype(jnp.bfloat16)

            @pl.when(h < heads - 1)
            def _():
                mine = partial(left)
                send_left(left).wait_recv()
                out_buf[left] = (mine + from_right[left].astype(jnp.float32)).astype(jnp.bfloat16)

            send_left(left).start()

    def finish(total):
        content = total[:, :KVL]
        inverse = lax.rsqrt(jnp.mean(content * content, axis=1, keepdims=True) + 1e-06)
        content = (content * inverse * gain_ref[...]).astype(jnp.bfloat16)
        e = total[:, KVL:]
        half = ROPE // 2
        swapped = jnp.concatenate([e[:, half:], e[:, :half]], axis=1)
        turned = (e * cos_ref[...] + swapped * sin_ref[...]).astype(jnp.bfloat16)
        mine = pl.ds(pl.multiple_of(h * cp, 16), cp)
        fresh = pl.ds(pl.multiple_of(h * pn, 16), pn)
        cache_ref[s, mine, :KVL] = content[:cp]
        cache_ref[s, mine, KVL:] = turned[:cp]
        new_ref[fresh, :KVL] = content[cp:]
        new_ref[fresh, KVL:] = turned[cp:]

    own = partial(h)

    @pl.when(h == 0)
    def _():
        send_left(h).wait_recv()
        finish(own + from_right[h].astype(jnp.float32))

    @pl.when(h == heads - 1)
    def _():
        send_right(h).wait_recv()
        finish(own + from_left[h].astype(jnp.float32))

    @pl.when((h > 0) & (h < heads - 1))
    def _():
        send_right(h).wait_recv()
        send_left(h).wait_recv()
        finish(own + from_left[h].astype(jnp.float32) + from_right[h].astype(jnp.float32))

    def block(source, c):
        return cache_ref.at[source, pl.ds(pl.multiple_of(c * cp, 16), cp), :]

    def gather_copies(c, side, where):
        fresh = new_ref.at[pl.ds(pl.multiple_of(c * pn, 16), pn), :]
        return [
            pltpu.make_async_remote_copy(
                src_ref=ref,
                dst_ref=ref,
                send_sem=ag_send.at[side, kind, c],
                recv_sem=ag_recv.at[kind, c],
                device_id=where,
                device_id_type=MESH,
            )
            for kind, ref in enumerate((block(s, c), fresh))
        ]

    def to_right(c):
        return gather_copies(c, 0, {"heads": h + 1})

    def to_left(c):
        return gather_copies(c, 1, {"heads": h - 1})

    def over(j, source, c):
        return pltpu.make_async_remote_copy(
            src_ref=block(source, c),
            dst_ref=block(source, c),
            send_sem=x_send.at[j - 1, c],
            recv_sem=x_recv.at[j - 1, c],
            device_id={"seq": lax.rem(s + 2 * j, seq)},
            device_id_type=MESH,
        )

    def across(source, c):
        return pltpu.make_async_remote_copy(
            src_ref=block(source, c),
            dst_ref=block(source, c),
            send_sem=sib_send.at[lax.div(source, 2), c],
            recv_sem=sib_recv.at[lax.div(source, 2), c],
            device_id={"seq": sibling},
            device_id_type=MESH,
        )

    def spread(c):
        for j in range(1, others + 1):
            over(j, s, c).start()
        across(s, c).start()

    @pl.when(h < heads - 1)
    def _():
        for copy in to_right(h):
            copy.start()

    @pl.when(h > 0)
    def _():
        for copy in to_left(h):
            copy.start()

    spread(h)
    for k in range(1, heads):

        @pl.when(h - k >= 0)
        def _():
            for copy in to_right(h - k):
                copy.wait_recv()

            @pl.when(h < heads - 1)
            def _():
                for copy in to_right(h - k):
                    copy.start()

            spread(h - k)

        @pl.when(h + k < heads)
        def _():
            for copy in to_left(h + k):
                copy.wait_recv()

            @pl.when(h > 0)
            def _():
                for copy in to_left(h + k):
                    copy.start()

            spread(h + k)

    def relay(c):
        for j in range(1, others + 1):
            source = lax.rem(s - 2 * j + seq, seq)
            over(j, source, c).wait_recv()
            across(source, c).start()

    relay(h)
    for k in range(1, heads):

        @pl.when(h - k >= 0)
        def _():
            relay(h - k)

        @pl.when(h + k < heads)
        def _():
            relay(h + k)

    for c in range(heads):
        for j in range(others + 1):
            across(lax.rem(sibling + 2 * j, seq), c).wait_recv()

    for c in range(heads):

        @pl.when(h != c)
        def _():
            send_right(c).wait_send()

        @pl.when((c <= h) & (h < heads - 1))
        def _():
            for copy in to_right(c):
                copy.wait_send()

        @pl.when((c >= h) & (h > 0))
        def _():
            for copy in to_left(c):
                copy.wait_send()

        for j in range(others + 1):
            across(lax.rem(s + 2 * j, seq), c).wait_send()
        for j in range(1, others + 1):
            over(j, s, c).wait_send()


def latent_rows(prompt_states, new_states, down_kv, gain_kv, cosine, sine):
    heads = lax.axis_size("heads")
    seq = lax.axis_size("seq")
    rows, fresh = prompt_states.shape[0], new_states.shape[0]
    width = down_kv.shape[1]
    chunk = rows // heads + fresh // heads
    others = max(seq // 2 - 1, 1)
    vmem = pl.BlockSpec(memory_space=pltpu.VMEM)
    dma = pltpu.SemaphoreType.DMA
    return pl.pallas_call(
        functools.partial(latent_kernel, heads, seq),
        out_shape=(
            jax.ShapeDtypeStruct((seq, rows, width), jnp.bfloat16),
            jax.ShapeDtypeStruct((fresh, width), jnp.bfloat16),
        ),
        in_specs=[vmem] * 6,
        out_specs=(vmem, vmem),
        scratch_shapes=[
            pltpu.VMEM((fresh, width), jnp.float32),
            pltpu.VMEM((heads, chunk, width), jnp.bfloat16),
            pltpu.VMEM((heads, chunk, width), jnp.bfloat16),
            pltpu.VMEM((heads, chunk, width), jnp.bfloat16),
            dma((heads,)),
            dma((heads,)),
            dma((heads,)),
            dma((2, 2, heads)),
            dma((2, heads)),
            dma((others, heads)),
            dma((others, heads)),
            dma((seq // 2, heads)),
            dma((seq // 2, heads)),
        ],
        compiler_params=pltpu.CompilerParams(
            collective_id=0, has_side_effects=True, vmem_limit_bytes=48 * 1024 * 1024
        ),
    )(prompt_states, new_states, down_kv, gain_kv[None, :], cosine, sine)


def per_device(
    prompt_states,
    new_states,
    prompt_lengths,
    routing,
    row_request,
    queries,
    gain_kv,
    down_kv,
    absorb_k,
    absorb_v,
    out_proj,
):
    owners = lax.axis_size("seq")
    own_index = lax.axis_index("seq")
    requests = prompt_lengths.shape[1]
    per_peer = requests // owners
    pr_rows = prompt_states.shape[0]
    dec_rows = new_states.shape[0]
    starts_all = jnp.cumsum(prompt_lengths, axis=1) - prompt_lengths
    my_lengths = prompt_lengths[own_index]
    my_starts = starts_all[own_index]
    row_ids = jnp.arange(pr_rows, dtype=jnp.int32)
    row_start = jnp.max(
        jnp.where(my_starts[None, :] <= row_ids[:, None], my_starts[None, :], 0), axis=1
    )
    prompt_pos = row_ids - row_start
    slot_ids = jnp.arange(requests, dtype=jnp.int32)
    source = slot_ids // per_peer
    slot_req = routing[source, own_index * per_peer + slot_ids % per_peer]
    slot_len = prompt_lengths[source, slot_req]
    token_ids = jnp.arange(dec_rows, dtype=jnp.int32)
    same_slot = row_request[:, None] == row_request[None, :]
    earlier = jnp.sum(
        (same_slot & (token_ids[:, None] > token_ids[None, :])).astype(jnp.int32), axis=1
    )
    row_len = slot_len[row_request]
    new_pos = row_len + earlier
    heads = lax.axis_size("heads")
    head_index = lax.axis_index("heads")
    cp = pr_rows // heads
    pn = 16 * -(-dec_rows // (16 * heads))
    padded = pn * heads - dec_rows
    my_pos = jnp.concatenate(
        [
            lax.dynamic_slice_in_dim(prompt_pos, head_index * cp, cp),
            lax.dynamic_slice_in_dim(jnp.pad(new_pos, (0, padded)), head_index * pn, pn),
        ]
    )
    cosine, sine = rotation_tables(my_pos)
    prompt_lat, new_lat = latent_rows(
        prompt_states, jnp.pad(new_states, ((0, padded), (0, 0))), down_kv, gain_kv, cosine, sine
    )
    new_lat = new_lat[:dec_rows]
    prompt_lat = prompt_lat.reshape(owners * pr_rows, -1)
    slot_first = source * pr_rows + starts_all[source, slot_req]
    offsets = jnp.arange(MAXLEN, dtype=jnp.int32)
    softmax_scale = 1.0 / math.sqrt(NOPE + ROPE)
    query_latent = jnp.einsum(
        "thn,hnc->thc", queries[:, :, :NOPE], absorb_k, preferred_element_type=jnp.float32
    ).astype(jnp.bfloat16)
    query_full = jnp.concatenate([query_latent, queries[:, :, NOPE:]], axis=2)
    row_first = slot_first[row_request]
    row_cache = prompt_lat[
        jnp.clip(row_first[:, None] + offsets[None, :], 0, owners * pr_rows - 1)
    ]
    cache_pos = jnp.arange(row_cache.shape[1], dtype=jnp.int32)
    score_cache = (
        jnp.einsum("thc,tpc->thp", query_full, row_cache, preferred_element_type=jnp.float32)
        * softmax_scale
    )
    score_new = (
        jnp.einsum("thc,uc->thu", query_full, new_lat, preferred_element_type=jnp.float32)
        * softmax_scale
    )
    ok_cache = (cache_pos[None, :] < row_len[:, None])[:, None, :]
    ok_new = (same_slot & (token_ids[None, :] <= token_ids[:, None]))[:, None, :]
    peak_score = jnp.maximum(
        jnp.max(jnp.where(ok_cache, score_cache, -jnp.inf), axis=2),
        jnp.max(jnp.where(ok_new, score_new, -jnp.inf), axis=2),
    )
    exp_cache = jnp.where(ok_cache, jnp.exp(score_cache - peak_score[:, :, None]), 0.0)
    exp_new = jnp.where(ok_new, jnp.exp(score_new - peak_score[:, :, None]), 0.0)
    denominator = jnp.sum(exp_cache, axis=2) + jnp.sum(exp_new, axis=2)
    weight_cache = (exp_cache / denominator[:, :, None]).astype(jnp.bfloat16)
    weight_new = (exp_new / denominator[:, :, None]).astype(jnp.bfloat16)
    latent_out = jnp.einsum(
        "thp,tpc->thc", weight_cache, row_cache[:, :, :KVL], preferred_element_type=jnp.float32
    )
    latent_out = latent_out + jnp.einsum(
        "thu,uc->thc", weight_new, new_lat[:, :KVL], preferred_element_type=jnp.float32
    )
    latent_out = latent_out.astype(jnp.bfloat16)
    head_out = jnp.einsum(
        "thc,hcv->thv", latent_out, absorb_v, preferred_element_type=jnp.float32
    ).astype(jnp.bfloat16)
    head_out = head_out.reshape(dec_rows, -1)
    projected = jnp.dot(
        lax.all_gather(head_out, "seq", axis=0, tiled=True),
        out_proj,
        preferred_element_type=jnp.float32,
    )
    return lax.psum_scatter(
        projected.astype(jnp.bfloat16), "heads", scatter_dimension=0, tiled=True
    )


def solution(mesh):
    return jax.shard_map(
        per_device,
        mesh=mesh,
        in_specs=(
            P(("groups", "seq"), "heads"),
            P(("groups", "seq"), "heads"),
            P("groups", None),
            P("groups", None),
            P(("groups", "seq")),
            P(("groups", "seq"), "heads", None),
            P(),
            P("heads", None),
            P("heads", None, None),
            P("heads", None, None),
            P("heads", "seq"),
        ),
        out_specs=P(("groups", "heads"), "seq"),
        check_vma=False,
    )
```

```python
import functools
import math

import jax
import jax.numpy as jnp
from jax import lax
from jax.experimental import pallas as pl
from jax.experimental.pallas import tpu as pltpu
from jax.sharding import PartitionSpec as P

KVL = 512
ROPE = 64
NOPE = 128
MAXLEN = 128


MESH = pl.DeviceIdType.MESH


def rotation_tables(positions):
    half = ROPE // 2
    order = jnp.arange(half, dtype=jnp.float32)
    freq = 10000.0 ** (-2.0 * order / ROPE)
    angle = positions.astype(jnp.float32)[:, None] * freq[None, :]
    cosine = jnp.cos(angle)
    sine = jnp.sin(angle)
    return (
        jnp.concatenate([cosine, cosine], axis=1),
        jnp.concatenate([-sine, sine], axis=1),
    )


def latent_kernel(
    heads,
    seq,
    x_ref,
    n_ref,
    w_ref,
    gain_ref,
    cos_ref,
    sin_ref,
    cache_ref,
    new_ref,
    new_part,
    out_buf,
    from_left,
    from_right,
    rs_send,
    rs_left,
    rs_right,
    ag_send,
    ag_recv,
    x_send,
    x_recv,
    sib_send,
    sib_recv,
):
    h = lax.axis_index("heads")
    s = lax.axis_index("seq")
    sibling = s + 1 - 2 * lax.rem(s, 2)
    cp = x_ref.shape[0] // heads
    pn = n_ref.shape[0] // heads
    others = seq // 2 - 1

    barrier = pltpu.get_barrier_semaphore()

    def greet(where):
        pl.semaphore_signal(barrier, inc=1, device_id=where, device_id_type=MESH)

    @pl.when(h > 0)
    def _():
        greet({"heads": h - 1})

    @pl.when(h < heads - 1)
    def _():
        greet({"heads": h + 1})

    greet({"seq": sibling})
    for j in range(1, others + 1):
        greet({"seq": lax.rem(s + 2 * j, seq)})
    pl.semaphore_wait(
        barrier,
        1 + others + jnp.where(h > 0, 1, 0) + jnp.where(h < heads - 1, 1, 0),
    )

    new_part[...] = jnp.dot(n_ref[...], w_ref[...], preferred_element_type=jnp.float32)

    def partial(c):
        rows = x_ref[pl.ds(pl.multiple_of(c * cp, 16), cp), :]
        top = jnp.dot(rows, w_ref[...], preferred_element_type=jnp.float32)
        return jnp.concatenate([top, new_part[pl.ds(pl.multiple_of(c * pn, 16), pn), :]], axis=0)

    def send_right(c):
        return pltpu.make_async_remote_copy(
            src_ref=out_buf.at[c],
            dst_ref=from_left.at[c],
            send_sem=rs_send.at[c],
            recv_sem=rs_left.at[c],
            device_id={"heads": h + 1},
            device_id_type=MESH,
        )

    def send_left(c):
        return pltpu.make_async_remote_copy(
            src_ref=out_buf.at[c],
            dst_ref=from_right.at[c],
            send_sem=rs_send.at[c],
            recv_sem=rs_right.at[c],
            device_id={"heads": h - 1},
            device_id_type=MESH,
        )

    for i in range(heads - 1):
        right, left = heads - 1 - i, i

        @pl.when(h < right)
        def _():
            @pl.when(h == 0)
            def _():
                out_buf[right] = partial(right).astype(jnp.bfloat16)

            @pl.when(h > 0)
            def _():
                mine = partial(right)
                send_right(right).wait_recv()
                out_buf[right] = (mine + from_left[right].astype(jnp.float32)).astype(jnp.bfloat16)

            send_right(right).start()

        @pl.when(h > left)
        def _():
            @pl.when(h == heads - 1)
            def _():
                out_buf[left] = partial(left).astype(jnp.bfloat16)

            @pl.when(h < heads - 1)
            def _():
                mine = partial(left)
                send_left(left).wait_recv()
                out_buf[left] = (mine + from_right[left].astype(jnp.float32)).astype(jnp.bfloat16)

            send_left(left).start()

    def finish(total):
        content = total[:, :KVL]
        inverse = lax.rsqrt(jnp.mean(content * content, axis=1, keepdims=True) + 1e-06)
        content = (content * inverse * gain_ref[...]).astype(jnp.bfloat16)
        e = total[:, KVL:]
        half = ROPE // 2
        swapped = jnp.concatenate([e[:, half:], e[:, :half]], axis=1)
        turned = (e * cos_ref[...] + swapped * sin_ref[...]).astype(jnp.bfloat16)
        mine = pl.ds(pl.multiple_of(h * cp, 16), cp)
        fresh = pl.ds(pl.multiple_of(h * pn, 16), pn)
        cache_ref[s, mine, :KVL] = content[:cp]
        cache_ref[s, mine, KVL:] = turned[:cp]
        new_ref[fresh, :KVL] = content[cp:]
        new_ref[fresh, KVL:] = turned[cp:]

    own = partial(h)

    @pl.when(h == 0)
    def _():
        send_left(h).wait_recv()
        finish(own + from_right[h].astype(jnp.float32))

    @pl.when(h == heads - 1)
    def _():
        send_right(h).wait_recv()
        finish(own + from_left[h].astype(jnp.float32))

    @pl.when((h > 0) & (h < heads - 1))
    def _():
        send_right(h).wait_recv()
        send_left(h).wait_recv()
        finish(own + from_left[h].astype(jnp.float32) + from_right[h].astype(jnp.float32))

    def block(source, c):
        return cache_ref.at[source, pl.ds(pl.multiple_of(c * cp, 16), cp), :]

    def gather_copies(c, side, where):
        fresh = new_ref.at[pl.ds(pl.multiple_of(c * pn, 16), pn), :]
        return [
            pltpu.make_async_remote_copy(
                src_ref=ref,
                dst_ref=ref,
                send_sem=ag_send.at[side, kind, c],
                recv_sem=ag_recv.at[kind, c],
                device_id=where,
                device_id_type=MESH,
            )
            for kind, ref in enumerate((block(s, c), fresh))
        ]

    def to_right(c):
        return gather_copies(c, 0, {"heads": h + 1})

    def to_left(c):
        return gather_copies(c, 1, {"heads": h - 1})

    def over(j, source, c):
        return pltpu.make_async_remote_copy(
            src_ref=block(source, c),
            dst_ref=block(source, c),
            send_sem=x_send.at[j - 1, c],
            recv_sem=x_recv.at[j - 1, c],
            device_id={"seq": lax.rem(s + 2 * j, seq)},
            device_id_type=MESH,
        )

    def across(source, c):
        return pltpu.make_async_remote_copy(
            src_ref=block(source, c),
            dst_ref=block(source, c),
            send_sem=sib_send.at[lax.div(source, 2), c],
            recv_sem=sib_recv.at[lax.div(source, 2), c],
            device_id={"seq": sibling},
            device_id_type=MESH,
        )

    def spread(c):
        for j in range(1, others + 1):
            over(j, s, c).start()
        across(s, c).start()

    @pl.when(h < heads - 1)
    def _():
        for copy in to_right(h):
            copy.start()

    @pl.when(h > 0)
    def _():
        for copy in to_left(h):
            copy.start()

    spread(h)
    for k in range(1, heads):

        @pl.when(h - k >= 0)
        def _():
            for copy in to_right(h - k):
                copy.wait_recv()

            @pl.when(h < heads - 1)
            def _():
                for copy in to_right(h - k):
                    copy.start()

            spread(h - k)

        @pl.when(h + k < heads)
        def _():
            for copy in to_left(h + k):
                copy.wait_recv()

            @pl.when(h > 0)
            def _():
                for copy in to_left(h + k):
                    copy.start()

            spread(h + k)

    def relay(c):
        for j in range(1, others + 1):
            source = lax.rem(s - 2 * j + seq, seq)
            over(j, source, c).wait_recv()
            across(source, c).start()

    relay(h)
    for k in range(1, heads):

        @pl.when(h - k >= 0)
        def _():
            relay(h - k)

        @pl.when(h + k < heads)
        def _():
            relay(h + k)

    for c in range(heads):
        for j in range(others + 1):
            across(lax.rem(sibling + 2 * j, seq), c).wait_recv()

    for c in range(heads):

        @pl.when(h != c)
        def _():
            send_right(c).wait_send()

        @pl.when((c <= h) & (h < heads - 1))
        def _():
            for copy in to_right(c):
                copy.wait_send()

        @pl.when((c >= h) & (h > 0))
        def _():
            for copy in to_left(c):
                copy.wait_send()

        for j in range(others + 1):
            across(lax.rem(s + 2 * j, seq), c).wait_send()
        for j in range(1, others + 1):
            over(j, s, c).wait_send()


def latent_rows(prompt_states, new_states, down_kv, gain_kv, cosine, sine):
    heads = lax.axis_size("heads")
    seq = lax.axis_size("seq")
    rows, fresh = prompt_states.shape[0], new_states.shape[0]
    width = down_kv.shape[1]
    chunk = rows // heads + fresh // heads
    others = max(seq // 2 - 1, 1)
    vmem = pl.BlockSpec(memory_space=pltpu.VMEM)
    dma = pltpu.SemaphoreType.DMA
    return pl.pallas_call(
        functools.partial(latent_kernel, heads, seq),
        out_shape=(
            jax.ShapeDtypeStruct((seq, rows, width), jnp.bfloat16),
            jax.ShapeDtypeStruct((fresh, width), jnp.bfloat16),
        ),
        in_specs=[vmem] * 6,
        out_specs=(vmem, vmem),
        scratch_shapes=[
            pltpu.VMEM((fresh, width), jnp.float32),
            pltpu.VMEM((heads, chunk, width), jnp.bfloat16),
            pltpu.VMEM((heads, chunk, width), jnp.bfloat16),
            pltpu.VMEM((heads, chunk, width), jnp.bfloat16),
            dma((heads,)),
            dma((heads,)),
            dma((heads,)),
            dma((2, 2, heads)),
            dma((2, heads)),
            dma((others, heads)),
            dma((others, heads)),
            dma((seq // 2, heads)),
            dma((seq // 2, heads)),
        ],
        compiler_params=pltpu.CompilerParams(
            collective_id=0, has_side_effects=True, vmem_limit_bytes=48 * 1024 * 1024
        ),
    )(prompt_states, new_states, down_kv, gain_kv[None, :], cosine, sine)


TOKENS = 4


def attend_kernel(start_ref, low_ref, len_ref, ql_ref, qr_ref, bias_ref, cache_ref, new_ref, out_ref):
    tokens = start_ref.shape[0]
    nh = ql_ref.shape[0] // tokens
    window = MAXLEN + 16
    scale = 1.0 / math.sqrt(NOPE + ROPE)
    contract = (((1,), (1,)), ((), ()))

    def scores(content, turned, keys):
        return (
            lax.dot_general(content, keys[:, :KVL], contract, preferred_element_type=jnp.float32)
            + lax.dot_general(turned, keys[:, KVL:], contract, preferred_element_type=jnp.float32)
        ) * scale

    def group(g, carry):
        rows = pl.ds(pl.multiple_of(g * (TOKENS * nh), TOKENS * nh), TOKENS * nh)
        content, turned = ql_ref[rows, :], qr_ref[rows, :]
        score_new = scores(content, turned, new_ref[...])
        held, weights_new = [], []
        for i in range(TOKENS):
            t = g * TOKENS + i
            low = low_ref[t]
            keys = cache_ref[pl.ds(pl.multiple_of(start_ref[t], 16), window), :]
            mine = slice(i * nh, (i + 1) * nh)
            score = scores(content[mine], turned[mine], keys)
            column = lax.broadcasted_iota(jnp.int32, score.shape, 1)
            usable = (column >= low) & (column < low + len_ref[t])
            score = jnp.where(usable, score, -jnp.inf)
            fresh = score_new[mine] + bias_ref[pl.ds(t, 1), :]
            peak = jnp.maximum(
                jnp.max(score, axis=1, keepdims=True), jnp.max(fresh, axis=1, keepdims=True)
            )
            score = jnp.exp(score - peak)
            fresh = jnp.exp(fresh - peak)
            total = jnp.sum(score, axis=1, keepdims=True) + jnp.sum(fresh, axis=1, keepdims=True)
            weights_new.append(fresh / total)
            held.append(
                jnp.dot(
                    (score / total).astype(jnp.bfloat16),
                    keys[:, :KVL],
                    preferred_element_type=jnp.float32,
                )
            )
        mixed = jnp.dot(
            jnp.concatenate(weights_new, axis=0).astype(jnp.bfloat16),
            new_ref[:, :KVL],
            preferred_element_type=jnp.float32,
        )
        out_ref[rows, :] = (jnp.concatenate(held, axis=0) + mixed).astype(jnp.bfloat16)
        return carry

    lax.fori_loop(0, tokens // TOKENS, group, 0)


def attend(start, low, length, ql, qr, bias, cache, new_lat):
    vmem = pl.BlockSpec(memory_space=pltpu.VMEM)
    smem = pl.BlockSpec(memory_space=pltpu.SMEM)
    return pl.pallas_call(
        attend_kernel,
        out_shape=jax.ShapeDtypeStruct(ql.shape, jnp.bfloat16),
        in_specs=[smem] * 3 + [vmem] * 5,
        out_specs=vmem,
        compiler_params=pltpu.CompilerParams(vmem_limit_bytes=48 * 1024 * 1024),
    )(start, low, length, ql, qr, bias, cache, new_lat)


PIECES = 2


def project_kernel(
    heads,
    seq,
    tile,
    ho_ref,
    w_hbm,
    out_ref,
    w_ref,
    gathered,
    total,
    out_buf,
    from_left,
    from_right,
    w_sem,
    x_send,
    x_recv,
    sib_send,
    sib_recv,
    rs_send,
    rs_left,
    rs_right,
):
    h = lax.axis_index("heads")
    s = lax.axis_index("seq")
    sibling = s + 1 - 2 * lax.rem(s, 2)
    others = seq // 2 - 1
    tokens, depth = ho_ref.shape
    width = w_ref.shape[1]
    tiles = width // tile
    piece = tokens // PIECES
    share = tokens * seq // heads

    def fetch(n):
        columns = pl.ds(n * tile, tile)
        return pltpu.make_async_copy(w_hbm.at[:, columns], w_ref.at[:, columns], w_sem.at[n])

    for n in range(tiles):
        fetch(n).start()

    barrier = pltpu.get_barrier_semaphore()

    def greet(where):
        pl.semaphore_signal(barrier, inc=1, device_id=where, device_id_type=MESH)

    @pl.when(h > 0)
    def _():
        greet({"heads": h - 1})

    @pl.when(h < heads - 1)
    def _():
        greet({"heads": h + 1})

    greet({"seq": sibling})
    for j in range(1, others + 1):
        greet({"seq": lax.rem(s + 2 * j, seq)})
    pl.semaphore_wait(
        barrier,
        1 + others + jnp.where(h > 0, 1, 0) + jnp.where(h < heads - 1, 1, 0),
    )

    def block(source, p):
        return gathered.at[source, pl.ds(p * piece, piece), :]

    def over(j, source, p):
        return pltpu.make_async_remote_copy(
            src_ref=ho_ref.at[pl.ds(p * piece, piece), :],
            dst_ref=block(source, p),
            send_sem=x_send.at[j - 1, p],
            recv_sem=x_recv.at[j - 1, p],
            device_id={"seq": lax.rem(s + 2 * j, seq)},
            device_id_type=MESH,
        )

    def across(source, p, own):
        return pltpu.make_async_remote_copy(
            src_ref=ho_ref.at[pl.ds(p * piece, piece), :] if own else block(source, p),
            dst_ref=block(source, p),
            send_sem=sib_send.at[lax.div(source, 2), p],
            recv_sem=sib_recv.at[lax.div(source, 2), p],
            device_id={"seq": sibling},
            device_id_type=MESH,
        )

    for p in range(PIECES):
        for j in range(1, others + 1):
            over(j, s, p).start()
        across(s, p, True).start()
    gathered[s] = ho_ref[...]
    for p in range(PIECES):
        for j in range(1, others + 1):
            source = lax.rem(s - 2 * j + seq, seq)
            over(j, source, p).wait_recv()
            across(source, p, False).start()
    for p in range(PIECES):
        for j in range(others + 1):
            across(lax.rem(sibling + 2 * j, seq), p, False).wait_recv()

    for n in range(tiles):
        fetch(n).wait()

    for n in range(tiles):
        rows = gathered[...].reshape(seq * tokens, depth)
        total[:, n * tile : (n + 1) * tile] = jnp.dot(
            rows, w_ref[:, n * tile : (n + 1) * tile], preferred_element_type=jnp.float32
        )

    def partial(c):
        return total[pl.ds(pl.multiple_of(c * share, 16), share), :]

    def send_right(c):
        return pltpu.make_async_remote_copy(
            src_ref=out_buf.at[c],
            dst_ref=from_left.at[c],
            send_sem=rs_send.at[c],
            recv_sem=rs_left.at[c],
            device_id={"heads": h + 1},
            device_id_type=MESH,
        )

    def send_left(c):
        return pltpu.make_async_remote_copy(
            src_ref=out_buf.at[c],
            dst_ref=from_right.at[c],
            send_sem=rs_send.at[c],
            recv_sem=rs_right.at[c],
            device_id={"heads": h - 1},
            device_id_type=MESH,
        )

    for i in range(heads - 1):
        right, left = heads - 1 - i, i

        @pl.when(h < right)
        def _():
            @pl.when(h == 0)
            def _():
                out_buf[right] = partial(right).astype(jnp.bfloat16)

            @pl.when(h > 0)
            def _():
                send_right(right).wait_recv()
                out_buf[right] = (
                    partial(right) + from_left[right].astype(jnp.float32)
                ).astype(jnp.bfloat16)

            send_right(right).start()

        @pl.when(h > left)
        def _():
            @pl.when(h == heads - 1)
            def _():
                out_buf[left] = partial(left).astype(jnp.bfloat16)

            @pl.when(h < heads - 1)
            def _():
                send_left(left).wait_recv()
                out_buf[left] = (
                    partial(left) + from_right[left].astype(jnp.float32)
                ).astype(jnp.bfloat16)

            send_left(left).start()

    @pl.when(h == 0)
    def _():
        send_left(h).wait_recv()
        out_ref[...] = (partial(h) + from_right[h].astype(jnp.float32)).astype(jnp.bfloat16)

    @pl.when(h == heads - 1)
    def _():
        send_right(h).wait_recv()
        out_ref[...] = (partial(h) + from_left[h].astype(jnp.float32)).astype(jnp.bfloat16)

    @pl.when((h > 0) & (h < heads - 1))
    def _():
        send_right(h).wait_recv()
        send_left(h).wait_recv()
        out_ref[...] = (
            partial(h) + from_left[h].astype(jnp.float32) + from_right[h].astype(jnp.float32)
        ).astype(jnp.bfloat16)

    for c in range(heads):

        @pl.when(h != c)
        def _():
            send_right(c).wait_send()

    for p in range(PIECES):
        for j in range(others + 1):
            across(lax.rem(s + 2 * j, seq), p, False).wait_send()
        for j in range(1, others + 1):
            over(j, s, p).wait_send()


def project(head_out, out_proj):
    heads = lax.axis_size("heads")
    seq = lax.axis_size("seq")
    tokens, depth = head_out.shape
    width = out_proj.shape[1]
    tile = 256 if width % 256 == 0 else width
    share = tokens * seq // heads
    others = max(seq // 2 - 1, 1)
    vmem = pl.BlockSpec(memory_space=pltpu.VMEM)
    dma = pltpu.SemaphoreType.DMA
    return pl.pallas_call(
        functools.partial(project_kernel, heads, seq, tile),
        out_shape=jax.ShapeDtypeStruct((share, width), jnp.bfloat16),
        in_specs=[vmem, pl.BlockSpec(memory_space=pl.ANY)],
        out_specs=vmem,
        scratch_shapes=[
            pltpu.VMEM((depth, width), jnp.bfloat16),
            pltpu.VMEM((seq, tokens, depth), jnp.bfloat16),
            pltpu.VMEM((seq * tokens, width), jnp.float32),
            pltpu.VMEM((heads, share, width), jnp.bfloat16),
            pltpu.VMEM((heads, share, width), jnp.bfloat16),
            pltpu.VMEM((heads, share, width), jnp.bfloat16),
            dma((width // tile,)),
            dma((others, PIECES)),
            dma((others, PIECES)),
            dma((seq // 2, PIECES)),
            dma((seq // 2, PIECES)),
            dma((heads,)),
            dma((heads,)),
            dma((heads,)),
        ],
        compiler_params=pltpu.CompilerParams(
            collective_id=1, has_side_effects=True, vmem_limit_bytes=56 * 1024 * 1024
        ),
    )(head_out, out_proj)


def per_device(
    prompt_states,
    new_states,
    prompt_lengths,
    routing,
    row_request,
    queries,
    gain_kv,
    down_kv,
    absorb_k,
    absorb_v,
    out_proj,
):
    owners = lax.axis_size("seq")
    own_index = lax.axis_index("seq")
    requests = prompt_lengths.shape[1]
    per_peer = requests // owners
    pr_rows = prompt_states.shape[0]
    dec_rows = new_states.shape[0]
    starts_all = jnp.cumsum(prompt_lengths, axis=1) - prompt_lengths
    my_lengths = prompt_lengths[own_index]
    my_starts = starts_all[own_index]
    row_ids = jnp.arange(pr_rows, dtype=jnp.int32)
    row_start = jnp.max(
        jnp.where(my_starts[None, :] <= row_ids[:, None], my_starts[None, :], 0), axis=1
    )
    prompt_pos = row_ids - row_start
    slot_ids = jnp.arange(requests, dtype=jnp.int32)
    source = slot_ids // per_peer
    slot_req = routing[source, own_index * per_peer + slot_ids % per_peer]
    slot_len = prompt_lengths[source, slot_req]
    token_ids = jnp.arange(dec_rows, dtype=jnp.int32)
    same_slot = row_request[:, None] == row_request[None, :]
    earlier = jnp.sum(
        (same_slot & (token_ids[:, None] > token_ids[None, :])).astype(jnp.int32), axis=1
    )
    row_len = slot_len[row_request]
    new_pos = row_len + earlier
    heads = lax.axis_size("heads")
    head_index = lax.axis_index("heads")
    cp = pr_rows // heads
    pn = 16 * -(-dec_rows // (16 * heads))
    padded = pn * heads - dec_rows
    my_pos = jnp.concatenate(
        [
            lax.dynamic_slice_in_dim(prompt_pos, head_index * cp, cp),
            lax.dynamic_slice_in_dim(jnp.pad(new_pos, (0, padded)), head_index * pn, pn),
        ]
    )
    cosine, sine = rotation_tables(my_pos)
    prompt_lat, new_lat = latent_rows(
        prompt_states, jnp.pad(new_states, ((0, padded), (0, 0))), down_kv, gain_kv, cosine, sine
    )
    new_lat = new_lat[:dec_rows]
    prompt_lat = prompt_lat.reshape(owners * pr_rows, -1)
    slot_first = source * pr_rows + starts_all[source, slot_req]
    query_latent = jnp.einsum(
        "thn,hnc->thc", queries[:, :, :NOPE], absorb_k, preferred_element_type=jnp.float32
    ).astype(jnp.bfloat16)
    row_first = slot_first[row_request]
    start = jnp.minimum(row_first // 16 * 16, owners * pr_rows - (MAXLEN + 16))
    bias = jnp.where(
        same_slot & (token_ids[None, :] <= token_ids[:, None]), jnp.float32(0), -jnp.inf
    )
    local_heads = queries.shape[1]
    latent_out = attend(
        start,
        row_first - start,
        row_len,
        query_latent.reshape(dec_rows * local_heads, KVL),
        queries[:, :, NOPE:].reshape(dec_rows * local_heads, ROPE),
        bias,
        prompt_lat,
        new_lat,
    ).reshape(dec_rows, local_heads, KVL)
    head_out = jnp.einsum(
        "thc,hcv->thv", latent_out, absorb_v, preferred_element_type=jnp.float32
    ).astype(jnp.bfloat16)
    head_out = head_out.reshape(dec_rows, -1)
    return project(head_out, out_proj)


def solution(mesh):
    return jax.shard_map(
        per_device,
        mesh=mesh,
        in_specs=(
            P(("groups", "seq"), "heads"),
            P(("groups", "seq"), "heads"),
            P("groups", None),
            P("groups", None),
            P(("groups", "seq")),
            P(("groups", "seq"), "heads", None),
            P(),
            P("heads", None),
            P("heads", None, None),
            P("heads", None, None),
            P("heads", "seq"),
        ),
        out_specs=P(("groups", "heads"), "seq"),
        check_vma=False,
    )
```

```python
import functools
import math

import jax
import jax.numpy as jnp
from jax import lax
from jax.experimental import pallas as pl
from jax.experimental.pallas import tpu as pltpu
from jax.sharding import PartitionSpec as P

KVL = 512
ROPE = 64
NOPE = 128
MAXLEN = 128


MESH = pl.DeviceIdType.MESH


def rotation_tables(positions):
    half = ROPE // 2
    order = jnp.arange(half, dtype=jnp.float32)
    freq = 10000.0 ** (-2.0 * order / ROPE)
    angle = positions.astype(jnp.float32)[:, None] * freq[None, :]
    cosine = jnp.cos(angle)
    sine = jnp.sin(angle)
    return (
        jnp.concatenate([cosine, cosine], axis=1),
        jnp.concatenate([-sine, sine], axis=1),
    )


def latent_kernel(
    heads,
    seq,
    x_ref,
    n_ref,
    w_ref,
    gain_ref,
    cos_ref,
    sin_ref,
    cache_ref,
    new_ref,
    new_part,
    out_buf,
    from_left,
    from_right,
    rs_send,
    rs_left,
    rs_right,
    ag_send,
    ag_recv,
    x_send,
    x_recv,
    sib_send,
    sib_recv,
):
    h = lax.axis_index("heads")
    s = lax.axis_index("seq")
    sibling = s + 1 - 2 * lax.rem(s, 2)
    cp = x_ref.shape[0] // heads
    pn = n_ref.shape[0] // heads
    others = seq // 2 - 1

    barrier = pltpu.get_barrier_semaphore()

    def greet(where):
        pl.semaphore_signal(barrier, inc=1, device_id=where, device_id_type=MESH)

    @pl.when(h > 0)
    def _():
        greet({"heads": h - 1})

    @pl.when(h < heads - 1)
    def _():
        greet({"heads": h + 1})

    greet({"seq": sibling})
    for j in range(1, others + 1):
        greet({"seq": lax.rem(s + 2 * j, seq)})
    pl.semaphore_wait(
        barrier,
        1 + others + jnp.where(h > 0, 1, 0) + jnp.where(h < heads - 1, 1, 0),
    )

    def compress(rows):
        return lax.dot_general(
            rows, w_ref[...], (((1,), (1,)), ((), ())), preferred_element_type=jnp.float32
        )

    new_part[...] = compress(n_ref[...])

    def partial(c):
        rows = x_ref[pl.ds(pl.multiple_of(c * cp, 16), cp), :]
        top = compress(rows)
        return jnp.concatenate([top, new_part[pl.ds(pl.multiple_of(c * pn, 16), pn), :]], axis=0)

    def send_right(c):
        return pltpu.make_async_remote_copy(
            src_ref=out_buf.at[c],
            dst_ref=from_left.at[c],
            send_sem=rs_send.at[c],
            recv_sem=rs_left.at[c],
            device_id={"heads": h + 1},
            device_id_type=MESH,
        )

    def send_left(c):
        return pltpu.make_async_remote_copy(
            src_ref=out_buf.at[c],
            dst_ref=from_right.at[c],
            send_sem=rs_send.at[c],
            recv_sem=rs_right.at[c],
            device_id={"heads": h - 1},
            device_id_type=MESH,
        )

    for i in range(heads - 1):
        right, left = heads - 1 - i, i

        @pl.when(h < right)
        def _():
            @pl.when(h == 0)
            def _():
                out_buf[right] = partial(right).astype(jnp.bfloat16)

            @pl.when(h > 0)
            def _():
                mine = partial(right)
                send_right(right).wait_recv()
                out_buf[right] = (mine + from_left[right].astype(jnp.float32)).astype(jnp.bfloat16)

            send_right(right).start()

        @pl.when(h > left)
        def _():
            @pl.when(h == heads - 1)
            def _():
                out_buf[left] = partial(left).astype(jnp.bfloat16)

            @pl.when(h < heads - 1)
            def _():
                mine = partial(left)
                send_left(left).wait_recv()
                out_buf[left] = (mine + from_right[left].astype(jnp.float32)).astype(jnp.bfloat16)

            send_left(left).start()

    def finish(total):
        content = total[:, :KVL]
        inverse = lax.rsqrt(jnp.mean(content * content, axis=1, keepdims=True) + 1e-06)
        content = (content * inverse * gain_ref[...]).astype(jnp.bfloat16)
        e = total[:, KVL:]
        half = ROPE // 2
        swapped = jnp.concatenate([e[:, half:], e[:, :half]], axis=1)
        turned = (e * cos_ref[...] + swapped * sin_ref[...]).astype(jnp.bfloat16)
        mine = pl.ds(pl.multiple_of(h * cp, 16), cp)
        fresh = pl.ds(pl.multiple_of(h * pn, 16), pn)
        cache_ref[s, mine, :KVL] = content[:cp]
        cache_ref[s, mine, KVL:] = turned[:cp]
        new_ref[fresh, :KVL] = content[cp:]
        new_ref[fresh, KVL:] = turned[cp:]

    own = partial(h)

    @pl.when(h == 0)
    def _():
        send_left(h).wait_recv()
        finish(own + from_right[h].astype(jnp.float32))

    @pl.when(h == heads - 1)
    def _():
        send_right(h).wait_recv()
        finish(own + from_left[h].astype(jnp.float32))

    @pl.when((h > 0) & (h < heads - 1))
    def _():
        send_right(h).wait_recv()
        send_left(h).wait_recv()
        finish(own + from_left[h].astype(jnp.float32) + from_right[h].astype(jnp.float32))

    def block(source, c):
        return cache_ref.at[source, pl.ds(pl.multiple_of(c * cp, 16), cp), :]

    def gather_copies(c, side, where):
        fresh = new_ref.at[pl.ds(pl.multiple_of(c * pn, 16), pn), :]
        return [
            pltpu.make_async_remote_copy(
                src_ref=ref,
                dst_ref=ref,
                send_sem=ag_send.at[side, kind, c],
                recv_sem=ag_recv.at[kind, c],
                device_id=where,
                device_id_type=MESH,
            )
            for kind, ref in enumerate((block(s, c), fresh))
        ]

    def to_right(c):
        return gather_copies(c, 0, {"heads": h + 1})

    def to_left(c):
        return gather_copies(c, 1, {"heads": h - 1})

    def over(j, source, c):
        return pltpu.make_async_remote_copy(
            src_ref=block(source, c),
            dst_ref=block(source, c),
            send_sem=x_send.at[j - 1, c],
            recv_sem=x_recv.at[j - 1, c],
            device_id={"seq": lax.rem(s + 2 * j, seq)},
            device_id_type=MESH,
        )

    def across(source, c):
        return pltpu.make_async_remote_copy(
            src_ref=block(source, c),
            dst_ref=block(source, c),
            send_sem=sib_send.at[lax.div(source, 2), c],
            recv_sem=sib_recv.at[lax.div(source, 2), c],
            device_id={"seq": sibling},
            device_id_type=MESH,
        )

    def spread(c):
        for j in range(1, others + 1):
            over(j, s, c).start()
        across(s, c).start()

    @pl.when(h < heads - 1)
    def _():
        for copy in to_right(h):
            copy.start()

    @pl.when(h > 0)
    def _():
        for copy in to_left(h):
            copy.start()

    spread(h)
    for k in range(1, heads):

        @pl.when(h - k >= 0)
        def _():
            for copy in to_right(h - k):
                copy.wait_recv()

            @pl.when(h < heads - 1)
            def _():
                for copy in to_right(h - k):
                    copy.start()

            spread(h - k)

        @pl.when(h + k < heads)
        def _():
            for copy in to_left(h + k):
                copy.wait_recv()

            @pl.when(h > 0)
            def _():
                for copy in to_left(h + k):
                    copy.start()

            spread(h + k)

    def relay(c):
        for j in range(1, others + 1):
            source = lax.rem(s - 2 * j + seq, seq)
            over(j, source, c).wait_recv()
            across(source, c).start()

    relay(h)
    for k in range(1, heads):

        @pl.when(h - k >= 0)
        def _():
            relay(h - k)

        @pl.when(h + k < heads)
        def _():
            relay(h + k)

    for c in range(heads):
        for j in range(others + 1):
            across(lax.rem(sibling + 2 * j, seq), c).wait_recv()

    for c in range(heads):

        @pl.when(h != c)
        def _():
            send_right(c).wait_send()

        @pl.when((c <= h) & (h < heads - 1))
        def _():
            for copy in to_right(c):
                copy.wait_send()

        @pl.when((c >= h) & (h > 0))
        def _():
            for copy in to_left(c):
                copy.wait_send()

        for j in range(others + 1):
            across(lax.rem(s + 2 * j, seq), c).wait_send()
        for j in range(1, others + 1):
            over(j, s, c).wait_send()


def latent_rows(prompt_states, new_states, down_kv, gain_kv, cosine, sine):
    heads = lax.axis_size("heads")
    seq = lax.axis_size("seq")
    rows, fresh = prompt_states.shape[0], new_states.shape[0]
    width = down_kv.shape[1]
    chunk = rows // heads + fresh // heads
    others = max(seq // 2 - 1, 1)
    vmem = pl.BlockSpec(memory_space=pltpu.VMEM)
    dma = pltpu.SemaphoreType.DMA
    return pl.pallas_call(
        functools.partial(latent_kernel, heads, seq),
        out_shape=(
            jax.ShapeDtypeStruct((seq, rows, width), jnp.bfloat16),
            jax.ShapeDtypeStruct((fresh, width), jnp.bfloat16),
        ),
        in_specs=[vmem] * 6,
        out_specs=(vmem, vmem),
        scratch_shapes=[
            pltpu.VMEM((fresh, width), jnp.float32),
            pltpu.VMEM((heads, chunk, width), jnp.bfloat16),
            pltpu.VMEM((heads, chunk, width), jnp.bfloat16),
            pltpu.VMEM((heads, chunk, width), jnp.bfloat16),
            dma((heads,)),
            dma((heads,)),
            dma((heads,)),
            dma((2, 2, heads)),
            dma((2, heads)),
            dma((others, heads)),
            dma((others, heads)),
            dma((seq // 2, heads)),
            dma((seq // 2, heads)),
        ],
        compiler_params=pltpu.CompilerParams(
            collective_id=0, has_side_effects=True, vmem_limit_bytes=48 * 1024 * 1024
        ),
    )(prompt_states, new_states, down_kv.T, gain_kv[None, :], cosine, sine)


TOKENS = 16


def attend_kernel(start_ref, low_ref, len_ref, ql_ref, qr_ref, bias_ref, cache_ref, new_ref, out_ref):
    tokens = start_ref.shape[0]
    nh = ql_ref.shape[0] // tokens
    window = MAXLEN + 16
    scale = 1.0 / math.sqrt(NOPE + ROPE)
    contract = (((1,), (1,)), ((), ()))

    def scores(content, turned, keys):
        return (
            lax.dot_general(content, keys[:, :KVL], contract, preferred_element_type=jnp.float32)
            + lax.dot_general(turned, keys[:, KVL:], contract, preferred_element_type=jnp.float32)
        ) * scale

    def group(g, carry):
        rows = pl.ds(pl.multiple_of(g * (TOKENS * nh), TOKENS * nh), TOKENS * nh)
        content, turned = ql_ref[rows, :], qr_ref[rows, :]
        spans = [slice(i * nh, (i + 1) * nh) for i in range(TOKENS)]
        column = lax.broadcasted_iota(jnp.int32, (nh, window), 1)
        keys, score, bias = [], [], []
        for i in range(TOKENS):
            t = g * TOKENS + i
            low = low_ref[t]
            keys.append(cache_ref[pl.ds(pl.multiple_of(start_ref[t], 16), window), :])
            usable = (column >= low) & (column < low + len_ref[t])
            score.append(
                jnp.where(usable, scores(content[spans[i]], turned[spans[i]], keys[i]), -jnp.inf)
            )
            bias.append(jnp.broadcast_to(bias_ref[pl.ds(t, 1), :], (nh, tokens)))
        score = jnp.concatenate(score, axis=0)
        fresh = scores(content, turned, new_ref[...]) + jnp.concatenate(bias, axis=0)
        peak = jnp.maximum(
            jnp.max(score, axis=1, keepdims=True), jnp.max(fresh, axis=1, keepdims=True)
        )
        score = jnp.exp(score - peak)
        fresh = jnp.exp(fresh - peak)
        inverse = 1.0 / (
            jnp.sum(score, axis=1, keepdims=True) + jnp.sum(fresh, axis=1, keepdims=True)
        )
        weights = (score * inverse).astype(jnp.bfloat16)
        held = [
            jnp.dot(weights[span], key[:, :KVL], preferred_element_type=jnp.float32)
            for span, key in zip(spans, keys)
        ]
        mixed = jnp.dot(
            (fresh * inverse).astype(jnp.bfloat16),
            new_ref[:, :KVL],
            preferred_element_type=jnp.float32,
        )
        out_ref[rows, :] = (jnp.concatenate(held, axis=0) + mixed).astype(jnp.bfloat16)
        return carry

    lax.fori_loop(0, tokens // TOKENS, group, 0)


def attend(start, low, length, ql, qr, bias, cache, new_lat):
    vmem = pl.BlockSpec(memory_space=pltpu.VMEM)
    smem = pl.BlockSpec(memory_space=pltpu.SMEM)
    return pl.pallas_call(
        attend_kernel,
        out_shape=jax.ShapeDtypeStruct(ql.shape, jnp.bfloat16),
        in_specs=[smem] * 3 + [vmem] * 5,
        out_specs=vmem,
        compiler_params=pltpu.CompilerParams(vmem_limit_bytes=48 * 1024 * 1024),
    )(start, low, length, ql, qr, bias, cache, new_lat)


PIECES = 2


def project_kernel(
    heads,
    seq,
    tile,
    spans,
    ho_ref,
    w_hbm,
    out_ref,
    w_ref,
    gathered,
    total,
    out_buf,
    from_left,
    from_right,
    w_sem,
    x_send,
    x_recv,
    sib_send,
    sib_recv,
    rs_send,
    rs_left,
    rs_right,
):
    h = lax.axis_index("heads")
    s = lax.axis_index("seq")
    sibling = s + 1 - 2 * lax.rem(s, 2)
    others = seq // 2 - 1
    tokens, depth = ho_ref.shape
    width = w_ref.shape[1]
    tiles = width // tile
    piece = tokens // PIECES
    share = tokens * seq // heads

    def fetch(n):
        columns = pl.ds(n * tile, tile)
        return pltpu.make_async_copy(w_hbm.at[:, columns], w_ref.at[:, columns], w_sem.at[n])

    for n in range(tiles):
        fetch(n).start()

    barrier = pltpu.get_barrier_semaphore()

    def greet(where):
        pl.semaphore_signal(barrier, inc=1, device_id=where, device_id_type=MESH)

    @pl.when(h > 0)
    def _():
        greet({"heads": h - 1})

    @pl.when(h < heads - 1)
    def _():
        greet({"heads": h + 1})

    greet({"seq": sibling})
    for j in range(1, others + 1):
        greet({"seq": lax.rem(s + 2 * j, seq)})
    pl.semaphore_wait(
        barrier,
        1 + others + jnp.where(h > 0, 1, 0) + jnp.where(h < heads - 1, 1, 0),
    )

    def block(source, p):
        return gathered.at[source, pl.ds(p * piece, piece), :]

    def over(j, source, p):
        return pltpu.make_async_remote_copy(
            src_ref=ho_ref.at[pl.ds(p * piece, piece), :],
            dst_ref=block(source, p),
            send_sem=x_send.at[j - 1, p],
            recv_sem=x_recv.at[j - 1, p],
            device_id={"seq": lax.rem(s + 2 * j, seq)},
            device_id_type=MESH,
        )

    def across(source, p, own):
        return pltpu.make_async_remote_copy(
            src_ref=ho_ref.at[pl.ds(p * piece, piece), :] if own else block(source, p),
            dst_ref=block(source, p),
            send_sem=sib_send.at[lax.div(source, 2), p],
            recv_sem=sib_recv.at[lax.div(source, 2), p],
            device_id={"seq": sibling},
            device_id_type=MESH,
        )

    for p in range(PIECES):
        for j in range(1, others + 1):
            over(j, s, p).start()
        across(s, p, True).start()
    gathered[s] = ho_ref[...]
    for p in range(PIECES):
        for j in range(1, others + 1):
            source = lax.rem(s - 2 * j + seq, seq)
            over(j, source, p).wait_recv()
            across(source, p, False).start()
    for p in range(PIECES):
        for j in range(others + 1):
            across(lax.rem(sibling + 2 * j, seq), p, False).wait_recv()

    def cut(q):
        return pl.ds(spans[q][0], spans[q][1])

    def partial(c, q):
        return total[pl.ds(pl.multiple_of(c * share, 16), share), cut(q)]

    def send_right(c, q):
        return pltpu.make_async_remote_copy(
            src_ref=out_buf.at[c, :, cut(q)],
            dst_ref=from_left.at[c, :, cut(q)],
            send_sem=rs_send.at[c, q],
            recv_sem=rs_left.at[c, q],
            device_id={"heads": h + 1},
            device_id_type=MESH,
        )

    def send_left(c, q):
        return pltpu.make_async_remote_copy(
            src_ref=out_buf.at[c, :, cut(q)],
            dst_ref=from_right.at[c, :, cut(q)],
            send_sem=rs_send.at[c, q],
            recv_sem=rs_right.at[c, q],
            device_id={"heads": h - 1},
            device_id_type=MESH,
        )

    for q, (low, size) in enumerate(spans):
        for n in range(low // tile, (low + size) // tile):
            fetch(n).wait()
            rows = gathered[...].reshape(seq * tokens, depth)
            total[:, n * tile : (n + 1) * tile] = jnp.dot(
                rows, w_ref[:, n * tile : (n + 1) * tile], preferred_element_type=jnp.float32
            )

        @pl.when(h == 0)
        def _():
            for c in range(heads - 1, 0, -1):
                out_buf[c, :, cut(q)] = partial(c, q).astype(jnp.bfloat16)
                send_right(c, q).start()

        @pl.when(h == heads - 1)
        def _():
            for c in range(heads - 1):
                out_buf[c, :, cut(q)] = partial(c, q).astype(jnp.bfloat16)
                send_left(c, q).start()

    for q in range(len(spans)):
        for i in range(heads - 1):
            right, left = heads - 1 - i, i

            @pl.when((h > 0) & (h < right))
            def _():
                send_right(right, q).wait_recv()
                out_buf[right, :, cut(q)] = (
                    partial(right, q) + from_left[right, :, cut(q)].astype(jnp.float32)
                ).astype(jnp.bfloat16)
                send_right(right, q).start()

            @pl.when((h > left) & (h < heads - 1))
            def _():
                send_left(left, q).wait_recv()
                out_buf[left, :, cut(q)] = (
                    partial(left, q) + from_right[left, :, cut(q)].astype(jnp.float32)
                ).astype(jnp.bfloat16)
                send_left(left, q).start()

    for q in range(len(spans)):

        @pl.when(h == 0)
        def _():
            send_left(h, q).wait_recv()
            out_ref[:, cut(q)] = (
                partial(h, q) + from_right[h, :, cut(q)].astype(jnp.float32)
            ).astype(jnp.bfloat16)

        @pl.when(h == heads - 1)
        def _():
            send_right(h, q).wait_recv()
            out_ref[:, cut(q)] = (
                partial(h, q) + from_left[h, :, cut(q)].astype(jnp.float32)
            ).astype(jnp.bfloat16)

        @pl.when((h > 0) & (h < heads - 1))
        def _():
            send_right(h, q).wait_recv()
            send_left(h, q).wait_recv()
            out_ref[:, cut(q)] = (
                partial(h, q)
                + from_left[h, :, cut(q)].astype(jnp.float32)
                + from_right[h, :, cut(q)].astype(jnp.float32)
            ).astype(jnp.bfloat16)

    for c in range(heads):

        @pl.when(h != c)
        def _():
            for q in range(len(spans)):
                send_right(c, q).wait_send()

    for p in range(PIECES):
        for j in range(others + 1):
            across(lax.rem(s + 2 * j, seq), p, False).wait_send()
        for j in range(1, others + 1):
            over(j, s, p).wait_send()


def project(head_out, out_proj):
    heads = lax.axis_size("heads")
    seq = lax.axis_size("seq")
    tokens, depth = head_out.shape
    width = out_proj.shape[1]
    tile = 256 if width % 256 == 0 else width
    middle = (width // tile + 1) // 2 * tile
    spans = [(0, middle), (middle, width - middle)] if middle < width else [(0, width)]
    share = tokens * seq // heads
    others = max(seq // 2 - 1, 1)
    vmem = pl.BlockSpec(memory_space=pltpu.VMEM)
    dma = pltpu.SemaphoreType.DMA
    return pl.pallas_call(
        functools.partial(project_kernel, heads, seq, tile, spans),
        out_shape=jax.ShapeDtypeStruct((share, width), jnp.bfloat16),
        in_specs=[vmem, pl.BlockSpec(memory_space=pl.ANY)],
        out_specs=vmem,
        scratch_shapes=[
            pltpu.VMEM((depth, width), jnp.bfloat16),
            pltpu.VMEM((seq, tokens, depth), jnp.bfloat16),
            pltpu.VMEM((seq * tokens, width), jnp.float32),
            pltpu.VMEM((heads, share, width), jnp.bfloat16),
            pltpu.VMEM((heads, share, width), jnp.bfloat16),
            pltpu.VMEM((heads, share, width), jnp.bfloat16),
            dma((width // tile,)),
            dma((others, PIECES)),
            dma((others, PIECES)),
            dma((seq // 2, PIECES)),
            dma((seq // 2, PIECES)),
            dma((heads, len(spans))),
            dma((heads, len(spans))),
            dma((heads, len(spans))),
        ],
        compiler_params=pltpu.CompilerParams(
            collective_id=1, has_side_effects=True, vmem_limit_bytes=56 * 1024 * 1024
        ),
    )(head_out, out_proj)


def per_device(
    prompt_states,
    new_states,
    prompt_lengths,
    routing,
    row_request,
    queries,
    gain_kv,
    down_kv,
    absorb_k,
    absorb_v,
    out_proj,
):
    owners = lax.axis_size("seq")
    own_index = lax.axis_index("seq")
    requests = prompt_lengths.shape[1]
    per_peer = requests // owners
    pr_rows = prompt_states.shape[0]
    dec_rows = new_states.shape[0]
    heads = lax.axis_size("heads")
    head_index = lax.axis_index("heads")
    cp = pr_rows // heads
    pn = 16 * -(-dec_rows // (16 * heads))
    padded = pn * heads - dec_rows
    request_ids = jnp.arange(requests, dtype=jnp.int32)
    starts_all = jnp.sum(
        jnp.where(
            request_ids[None, None, :] < request_ids[None, :, None],
            prompt_lengths[:, None, :],
            0,
        ),
        axis=2,
    )
    my_starts = lax.dynamic_slice_in_dim(starts_all, own_index, 1)
    row_ids = head_index * cp + jnp.arange(cp, dtype=jnp.int32)
    row_start = jnp.max(
        jnp.where(my_starts <= row_ids[:, None], my_starts, 0), axis=1
    )
    prompt_pos = row_ids - row_start
    source = request_ids // per_peer
    slot_req = lax.dynamic_slice_in_dim(
        routing.reshape(owners, owners, per_peer), own_index, 1, axis=1
    ).reshape(requests)
    chosen = slot_req[:, None] == request_ids[None, :]
    slot_len = jnp.sum(
        jnp.where(chosen, jnp.repeat(prompt_lengths, per_peer, axis=0), 0), axis=1
    )
    slot_first = source * pr_rows + jnp.sum(
        jnp.where(chosen, jnp.repeat(starts_all, per_peer, axis=0), 0), axis=1
    )
    token_ids = jnp.arange(dec_rows, dtype=jnp.int32)
    same_slot = row_request[:, None] == row_request[None, :]
    earlier = jnp.sum(
        (same_slot & (token_ids[:, None] > token_ids[None, :])).astype(jnp.int32), axis=1
    )
    row_slot = row_request[:, None] == request_ids[None, :]
    row_len = jnp.sum(jnp.where(row_slot, slot_len[None, :], 0), axis=1)
    row_first = jnp.sum(jnp.where(row_slot, slot_first[None, :], 0), axis=1)
    new_pos = row_len + earlier
    my_pos = jnp.concatenate(
        [
            prompt_pos,
            lax.dynamic_slice_in_dim(jnp.pad(new_pos, (0, padded)), head_index * pn, pn),
        ]
    )
    cosine, sine = rotation_tables(my_pos)
    prompt_lat, new_lat = latent_rows(
        prompt_states, jnp.pad(new_states, ((0, padded), (0, 0))), down_kv, gain_kv, cosine, sine
    )
    new_lat = new_lat[:dec_rows]
    prompt_lat = prompt_lat.reshape(owners * pr_rows, -1)
    query_latent = jnp.einsum(
        "thn,hnc->thc", queries[:, :, :NOPE], absorb_k, preferred_element_type=jnp.float32
    ).astype(jnp.bfloat16)
    start = jnp.minimum(row_first // 16 * 16, owners * pr_rows - (MAXLEN + 16))
    bias = jnp.where(
        same_slot & (token_ids[None, :] <= token_ids[:, None]), jnp.float32(0), -jnp.inf
    )
    local_heads = queries.shape[1]
    latent_out = attend(
        start,
        row_first - start,
        row_len,
        query_latent.reshape(dec_rows * local_heads, KVL),
        queries[:, :, NOPE:].reshape(dec_rows * local_heads, ROPE),
        bias,
        prompt_lat,
        new_lat,
    ).reshape(dec_rows, local_heads, KVL)
    head_out = jnp.einsum(
        "thc,hcv->thv", latent_out, absorb_v, preferred_element_type=jnp.float32
    ).astype(jnp.bfloat16)
    head_out = head_out.reshape(dec_rows, -1)
    return project(head_out, out_proj)


def solution(mesh):
    return jax.shard_map(
        per_device,
        mesh=mesh,
        in_specs=(
            P(("groups", "seq"), "heads"),
            P(("groups", "seq"), "heads"),
            P("groups", None),
            P("groups", None),
            P(("groups", "seq")),
            P(("groups", "seq"), "heads", None),
            P(),
            P("heads", None),
            P("heads", None, None),
            P("heads", None, None),
            P("heads", "seq"),
        ),
        out_specs=P(("groups", "heads"), "seq"),
        check_vma=False,
    )
```

```python
import functools
import math

import jax
import jax.numpy as jnp
from jax import lax
from jax.experimental import pallas as pl
from jax.experimental.pallas import tpu as pltpu
from jax.sharding import PartitionSpec as P

KVL = 512
ROPE = 64
NOPE = 128
MAXLEN = 128


MESH = pl.DeviceIdType.MESH


def rotation_tables(positions):
    half = ROPE // 2
    order = jnp.arange(half, dtype=jnp.float32)
    freq = 10000.0 ** (-2.0 * order / ROPE)
    angle = positions.astype(jnp.float32)[:, None] * freq[None, :]
    cosine = jnp.cos(angle)
    sine = jnp.sin(angle)
    return (
        jnp.concatenate([cosine, cosine], axis=1),
        jnp.concatenate([-sine, sine], axis=1),
    )


def latent_kernel(
    heads,
    seq,
    x_ref,
    n_ref,
    w_ref,
    gain_ref,
    cos_ref,
    sin_ref,
    cache_ref,
    new_ref,
    new_part,
    out_buf,
    from_left,
    from_right,
    rs_send,
    rs_left,
    rs_right,
    ag_send,
    ag_recv,
    x_send,
    x_recv,
    sib_send,
    sib_recv,
):
    h = lax.axis_index("heads")
    s = lax.axis_index("seq")
    sibling = s + 1 - 2 * lax.rem(s, 2)
    cp = x_ref.shape[0] // heads
    pn = n_ref.shape[0] // heads
    others = seq // 2 - 1

    barrier = pltpu.get_barrier_semaphore()

    def greet(where):
        pl.semaphore_signal(barrier, inc=1, device_id=where, device_id_type=MESH)

    @pl.when(h > 0)
    def _():
        greet({"heads": h - 1})

    @pl.when(h < heads - 1)
    def _():
        greet({"heads": h + 1})

    greet({"seq": sibling})
    for j in range(1, others + 1):
        greet({"seq": lax.rem(s + 2 * j, seq)})
    pl.semaphore_wait(
        barrier,
        1 + others + jnp.where(h > 0, 1, 0) + jnp.where(h < heads - 1, 1, 0),
    )

    def compress(rows):
        return lax.dot_general(
            rows, w_ref[...], (((1,), (1,)), ((), ())), preferred_element_type=jnp.float32
        )

    new_part[...] = compress(n_ref[...])

    def partial(c):
        rows = x_ref[pl.ds(pl.multiple_of(c * cp, 16), cp), :]
        top = compress(rows)
        return jnp.concatenate([top, new_part[pl.ds(pl.multiple_of(c * pn, 16), pn), :]], axis=0)

    def send_right(c):
        return pltpu.make_async_remote_copy(
            src_ref=out_buf.at[c],
            dst_ref=from_left.at[c],
            send_sem=rs_send.at[c],
            recv_sem=rs_left.at[c],
            device_id={"heads": h + 1},
            device_id_type=MESH,
        )

    def send_left(c):
        return pltpu.make_async_remote_copy(
            src_ref=out_buf.at[c],
            dst_ref=from_right.at[c],
            send_sem=rs_send.at[c],
            recv_sem=rs_right.at[c],
            device_id={"heads": h - 1},
            device_id_type=MESH,
        )

    for i in range(heads - 1):
        right, left = heads - 1 - i, i

        @pl.when(h < right)
        def _():
            @pl.when(h == 0)
            def _():
                out_buf[right] = partial(right).astype(jnp.bfloat16)

            @pl.when(h > 0)
            def _():
                mine = partial(right)
                send_right(right).wait_recv()
                out_buf[right] = (mine + from_left[right].astype(jnp.float32)).astype(jnp.bfloat16)

            send_right(right).start()

        @pl.when(h > left)
        def _():
            @pl.when(h == heads - 1)
            def _():
                out_buf[left] = partial(left).astype(jnp.bfloat16)

            @pl.when(h < heads - 1)
            def _():
                mine = partial(left)
                send_left(left).wait_recv()
                out_buf[left] = (mine + from_right[left].astype(jnp.float32)).astype(jnp.bfloat16)

            send_left(left).start()

    def finish(total):
        content = total[:, :KVL]
        inverse = lax.rsqrt(jnp.mean(content * content, axis=1, keepdims=True) + 1e-06)
        content = (content * inverse * gain_ref[...]).astype(jnp.bfloat16)
        e = total[:, KVL:]
        half = ROPE // 2
        swapped = jnp.concatenate([e[:, half:], e[:, :half]], axis=1)
        turned = (e * cos_ref[...] + swapped * sin_ref[...]).astype(jnp.bfloat16)
        mine = pl.ds(pl.multiple_of(h * cp, 16), cp)
        fresh = pl.ds(pl.multiple_of(h * pn, 16), pn)
        cache_ref[s, mine, :KVL] = content[:cp]
        cache_ref[s, mine, KVL:] = turned[:cp]
        new_ref[fresh, :KVL] = content[cp:]
        new_ref[fresh, KVL:] = turned[cp:]

    own = partial(h)

    @pl.when(h == 0)
    def _():
        send_left(h).wait_recv()
        finish(own + from_right[h].astype(jnp.float32))

    @pl.when(h == heads - 1)
    def _():
        send_right(h).wait_recv()
        finish(own + from_left[h].astype(jnp.float32))

    @pl.when((h > 0) & (h < heads - 1))
    def _():
        send_right(h).wait_recv()
        send_left(h).wait_recv()
        finish(own + from_left[h].astype(jnp.float32) + from_right[h].astype(jnp.float32))

    def block(source, c):
        return cache_ref.at[source, pl.ds(pl.multiple_of(c * cp, 16), cp), :]

    def gather_copies(c, side, where):
        fresh = new_ref.at[pl.ds(pl.multiple_of(c * pn, 16), pn), :]
        return [
            pltpu.make_async_remote_copy(
                src_ref=ref,
                dst_ref=ref,
                send_sem=ag_send.at[side, kind, c],
                recv_sem=ag_recv.at[kind, c],
                device_id=where,
                device_id_type=MESH,
            )
            for kind, ref in enumerate((block(s, c), fresh))
        ]

    def to_right(c):
        return gather_copies(c, 0, {"heads": h + 1})

    def to_left(c):
        return gather_copies(c, 1, {"heads": h - 1})

    def over(j, source, c):
        return pltpu.make_async_remote_copy(
            src_ref=block(source, c),
            dst_ref=block(source, c),
            send_sem=x_send.at[j - 1, c],
            recv_sem=x_recv.at[j - 1, c],
            device_id={"seq": lax.rem(s + 2 * j, seq)},
            device_id_type=MESH,
        )

    def across(source, c):
        return pltpu.make_async_remote_copy(
            src_ref=block(source, c),
            dst_ref=block(source, c),
            send_sem=sib_send.at[lax.div(source, 2), c],
            recv_sem=sib_recv.at[lax.div(source, 2), c],
            device_id={"seq": sibling},
            device_id_type=MESH,
        )

    def spread(c):
        for j in range(1, others + 1):
            over(j, s, c).start()
        across(s, c).start()

    @pl.when(h < heads - 1)
    def _():
        for copy in to_right(h):
            copy.start()

    @pl.when(h > 0)
    def _():
        for copy in to_left(h):
            copy.start()

    spread(h)
    for k in range(1, heads):

        @pl.when(h - k >= 0)
        def _():
            for copy in to_right(h - k):
                copy.wait_recv()

            @pl.when(h < heads - 1)
            def _():
                for copy in to_right(h - k):
                    copy.start()

            spread(h - k)

        @pl.when(h + k < heads)
        def _():
            for copy in to_left(h + k):
                copy.wait_recv()

            @pl.when(h > 0)
            def _():
                for copy in to_left(h + k):
                    copy.start()

            spread(h + k)

    def relay(c):
        for j in range(1, others + 1):
            source = lax.rem(s - 2 * j + seq, seq)
            over(j, source, c).wait_recv()
            across(source, c).start()

    relay(h)
    for k in range(1, heads):

        @pl.when(h - k >= 0)
        def _():
            relay(h - k)

        @pl.when(h + k < heads)
        def _():
            relay(h + k)

    for c in range(heads):
        for j in range(others + 1):
            across(lax.rem(sibling + 2 * j, seq), c).wait_recv()

    for c in range(heads):

        @pl.when(h != c)
        def _():
            send_right(c).wait_send()

        @pl.when((c <= h) & (h < heads - 1))
        def _():
            for copy in to_right(c):
                copy.wait_send()

        @pl.when((c >= h) & (h > 0))
        def _():
            for copy in to_left(c):
                copy.wait_send()

        for j in range(others + 1):
            across(lax.rem(s + 2 * j, seq), c).wait_send()
        for j in range(1, others + 1):
            over(j, s, c).wait_send()


def latent_rows(prompt_states, new_states, down_kv, gain_kv, cosine, sine):
    heads = lax.axis_size("heads")
    seq = lax.axis_size("seq")
    rows, fresh = prompt_states.shape[0], new_states.shape[0]
    width = down_kv.shape[1]
    chunk = rows // heads + fresh // heads
    others = max(seq // 2 - 1, 1)
    vmem = pl.BlockSpec(memory_space=pltpu.VMEM)
    dma = pltpu.SemaphoreType.DMA
    return pl.pallas_call(
        functools.partial(latent_kernel, heads, seq),
        out_shape=(
            jax.ShapeDtypeStruct((seq, rows, width), jnp.bfloat16),
            jax.ShapeDtypeStruct((fresh, width), jnp.bfloat16),
        ),
        in_specs=[vmem] * 6,
        out_specs=(vmem, vmem),
        scratch_shapes=[
            pltpu.VMEM((fresh, width), jnp.float32),
            pltpu.VMEM((heads, chunk, width), jnp.bfloat16),
            pltpu.VMEM((heads, chunk, width), jnp.bfloat16),
            pltpu.VMEM((heads, chunk, width), jnp.bfloat16),
            dma((heads,)),
            dma((heads,)),
            dma((heads,)),
            dma((2, 2, heads)),
            dma((2, heads)),
            dma((others, heads)),
            dma((others, heads)),
            dma((seq // 2, heads)),
            dma((seq // 2, heads)),
        ],
        compiler_params=pltpu.CompilerParams(
            collective_id=0, has_side_effects=True, vmem_limit_bytes=48 * 1024 * 1024
        ),
    )(prompt_states, new_states, down_kv.T, gain_kv[None, :], cosine, sine)


TOKENS = 16


def attend_kernel(start_ref, low_ref, len_ref, ql_ref, qr_ref, bias_ref, cache_ref, new_ref, out_ref):
    tokens = start_ref.shape[0]
    nh = ql_ref.shape[0] // tokens
    window = MAXLEN + 16
    scale = 1.0 / math.sqrt(NOPE + ROPE)
    contract = (((1,), (1,)), ((), ()))

    def scores(content, turned, keys):
        return (
            lax.dot_general(content, keys[:, :KVL], contract, preferred_element_type=jnp.float32)
            + lax.dot_general(turned, keys[:, KVL:], contract, preferred_element_type=jnp.float32)
        ) * scale

    def group(g, carry):
        rows = pl.ds(pl.multiple_of(g * (TOKENS * nh), TOKENS * nh), TOKENS * nh)
        content, turned = ql_ref[rows, :], qr_ref[rows, :]
        spans = [slice(i * nh, (i + 1) * nh) for i in range(TOKENS)]
        column = lax.broadcasted_iota(jnp.int32, (nh, window), 1)
        keys, score, bias = [], [], []
        for i in range(TOKENS):
            t = g * TOKENS + i
            low = low_ref[t]
            keys.append(cache_ref[pl.ds(pl.multiple_of(start_ref[t], 16), window), :])
            usable = (column >= low) & (column < low + len_ref[t])
            score.append(
                jnp.where(usable, scores(content[spans[i]], turned[spans[i]], keys[i]), -jnp.inf)
            )
            bias.append(jnp.broadcast_to(bias_ref[pl.ds(t, 1), :], (nh, tokens)))
        score = jnp.concatenate(score, axis=0)
        fresh = scores(content, turned, new_ref[...]) + jnp.concatenate(bias, axis=0)
        peak = jnp.maximum(
            jnp.max(score, axis=1, keepdims=True), jnp.max(fresh, axis=1, keepdims=True)
        )
        score = jnp.exp(score - peak)
        fresh = jnp.exp(fresh - peak)
        inverse = 1.0 / (
            jnp.sum(score, axis=1, keepdims=True) + jnp.sum(fresh, axis=1, keepdims=True)
        )
        weights = (score * inverse).astype(jnp.bfloat16)
        held = [
            jnp.dot(weights[span], key[:, :KVL], preferred_element_type=jnp.float32)
            for span, key in zip(spans, keys)
        ]
        mixed = jnp.dot(
            (fresh * inverse).astype(jnp.bfloat16),
            new_ref[:, :KVL],
            preferred_element_type=jnp.float32,
        )
        out_ref[rows, :] = (jnp.concatenate(held, axis=0) + mixed).astype(jnp.bfloat16)
        return carry

    lax.fori_loop(0, tokens // TOKENS, group, 0)


def attend(start, low, length, ql, qr, bias, cache, new_lat):
    vmem = pl.BlockSpec(memory_space=pltpu.VMEM)
    smem = pl.BlockSpec(memory_space=pltpu.SMEM)
    return pl.pallas_call(
        attend_kernel,
        out_shape=jax.ShapeDtypeStruct(ql.shape, jnp.bfloat16),
        in_specs=[smem] * 3 + [vmem] * 5,
        out_specs=vmem,
        compiler_params=pltpu.CompilerParams(vmem_limit_bytes=48 * 1024 * 1024),
    )(start, low, length, ql, qr, bias, cache, new_lat)


PIECES = 2


def project_kernel(
    heads,
    seq,
    tile,
    spans,
    ho_ref,
    w_hbm,
    out_ref,
    w_ref,
    gathered,
    total,
    out_buf,
    from_left,
    from_right,
    w_sem,
    x_send,
    x_recv,
    sib_send,
    sib_recv,
    rs_send,
    rs_left,
    rs_right,
):
    h = lax.axis_index("heads")
    s = lax.axis_index("seq")
    sibling = s + 1 - 2 * lax.rem(s, 2)
    others = seq // 2 - 1
    tokens, depth = ho_ref.shape
    width = w_ref.shape[1]
    tiles = width // tile
    piece = tokens // PIECES
    share = tokens * seq // heads

    def fetch(n):
        columns = pl.ds(n * tile, tile)
        return pltpu.make_async_copy(w_hbm.at[:, columns], w_ref.at[:, columns], w_sem.at[n])

    for n in range(tiles):
        fetch(n).start()

    barrier = pltpu.get_barrier_semaphore()

    def greet(where):
        pl.semaphore_signal(barrier, inc=1, device_id=where, device_id_type=MESH)

    @pl.when(h > 0)
    def _():
        greet({"heads": h - 1})

    @pl.when(h < heads - 1)
    def _():
        greet({"heads": h + 1})

    greet({"seq": sibling})
    for j in range(1, others + 1):
        greet({"seq": lax.rem(s + 2 * j, seq)})
    pl.semaphore_wait(
        barrier,
        1 + others + jnp.where(h > 0, 1, 0) + jnp.where(h < heads - 1, 1, 0),
    )

    def block(source, p):
        return gathered.at[source, pl.ds(p * piece, piece), :]

    def over(j, source, p):
        return pltpu.make_async_remote_copy(
            src_ref=ho_ref.at[pl.ds(p * piece, piece), :],
            dst_ref=block(source, p),
            send_sem=x_send.at[j - 1, p],
            recv_sem=x_recv.at[j - 1, p],
            device_id={"seq": lax.rem(s + 2 * j, seq)},
            device_id_type=MESH,
        )

    def across(source, p, own):
        return pltpu.make_async_remote_copy(
            src_ref=ho_ref.at[pl.ds(p * piece, piece), :] if own else block(source, p),
            dst_ref=block(source, p),
            send_sem=sib_send.at[lax.div(source, 2), p],
            recv_sem=sib_recv.at[lax.div(source, 2), p],
            device_id={"seq": sibling},
            device_id_type=MESH,
        )

    for p in range(PIECES):
        for j in range(1, others + 1):
            over(j, s, p).start()
        across(s, p, True).start()
    gathered[s] = ho_ref[...]
    for p in range(PIECES):
        across(sibling, p, False).wait_recv()

    def cut(q):
        return pl.ds(spans[q][0], spans[q][1])

    def partial(c, q):
        return total[pl.ds(pl.multiple_of(c * share, 16), share), cut(q)]

    def send_right(c, q):
        return pltpu.make_async_remote_copy(
            src_ref=out_buf.at[c, :, cut(q)],
            dst_ref=from_left.at[c, :, cut(q)],
            send_sem=rs_send.at[c, q],
            recv_sem=rs_left.at[c, q],
            device_id={"heads": h + 1},
            device_id_type=MESH,
        )

    def send_left(c, q):
        return pltpu.make_async_remote_copy(
            src_ref=out_buf.at[c, :, cut(q)],
            dst_ref=from_right.at[c, :, cut(q)],
            send_sem=rs_send.at[c, q],
            recv_sem=rs_right.at[c, q],
            device_id={"heads": h - 1},
            device_id_type=MESH,
        )

    per_chip = 2 * tokens // share

    def chip_of(j):
        return lax.rem(lax.div(s, 2) + j, seq // 2)

    def multiply(j):
        chip = chip_of(j)
        rows = gathered[pl.ds(2 * chip, 2)].reshape(2 * tokens, depth)
        place = pl.ds(pl.multiple_of(chip * 2 * tokens, 16), 2 * tokens)
        for q, (low, size) in enumerate(spans):
            for n in range(low // tile, (low + size) // tile):
                if j == 0:
                    fetch(n).wait()
                total[place, n * tile : (n + 1) * tile] = jnp.dot(
                    rows, w_ref[:, n * tile : (n + 1) * tile], preferred_element_type=jnp.float32
                )
            for k in range(per_chip):
                c = chip * per_chip + k

                @pl.when((h == 0) & (c > 0))
                def _():
                    out_buf[c, :, cut(q)] = partial(c, q).astype(jnp.bfloat16)
                    send_right(c, q).start()

                @pl.when((h == heads - 1) & (c < heads - 1))
                def _():
                    out_buf[c, :, cut(q)] = partial(c, q).astype(jnp.bfloat16)
                    send_left(c, q).start()

    def reduce(j):
        for q in range(len(spans)):
            for k in range(per_chip):
                c = chip_of(j) * per_chip + k

                @pl.when((h > 0) & (h < c))
                def _():
                    send_right(c, q).wait_recv()
                    out_buf[c, :, cut(q)] = (
                        partial(c, q) + from_left[c, :, cut(q)].astype(jnp.float32)
                    ).astype(jnp.bfloat16)
                    send_right(c, q).start()

                @pl.when((h > c) & (h < heads - 1))
                def _():
                    send_left(c, q).wait_recv()
                    out_buf[c, :, cut(q)] = (
                        partial(c, q) + from_right[c, :, cut(q)].astype(jnp.float32)
                    ).astype(jnp.bfloat16)
                    send_left(c, q).start()

    multiply(0)
    for j in range(1, others + 1):
        for p in range(PIECES):
            source = lax.rem(s - 2 * j + seq, seq)
            over(j, source, p).wait_recv()
            across(source, p, False).start()
    reduce(0)
    for j in range(1, others + 1):
        for p in range(PIECES):
            across(lax.rem(sibling + 2 * j, seq), p, False).wait_recv()
    for j in range(1, others + 1):
        multiply(j)
        reduce(j)

    for q in range(len(spans)):

        @pl.when(h == 0)
        def _():
            send_left(h, q).wait_recv()
            out_ref[:, cut(q)] = (
                partial(h, q) + from_right[h, :, cut(q)].astype(jnp.float32)
            ).astype(jnp.bfloat16)

        @pl.when(h == heads - 1)
        def _():
            send_right(h, q).wait_recv()
            out_ref[:, cut(q)] = (
                partial(h, q) + from_left[h, :, cut(q)].astype(jnp.float32)
            ).astype(jnp.bfloat16)

        @pl.when((h > 0) & (h < heads - 1))
        def _():
            send_right(h, q).wait_recv()
            send_left(h, q).wait_recv()
            out_ref[:, cut(q)] = (
                partial(h, q)
                + from_left[h, :, cut(q)].astype(jnp.float32)
                + from_right[h, :, cut(q)].astype(jnp.float32)
            ).astype(jnp.bfloat16)

    for c in range(heads):

        @pl.when(h != c)
        def _():
            for q in range(len(spans)):
                send_right(c, q).wait_send()

    for p in range(PIECES):
        for j in range(others + 1):
            across(lax.rem(s + 2 * j, seq), p, False).wait_send()
        for j in range(1, others + 1):
            over(j, s, p).wait_send()


def project(head_out, out_proj):
    heads = lax.axis_size("heads")
    seq = lax.axis_size("seq")
    tokens, depth = head_out.shape
    width = out_proj.shape[1]
    tile = 256 if width % 256 == 0 else width
    middle = (width // tile + 1) // 2 * tile
    spans = [(0, middle), (middle, width - middle)] if middle < width else [(0, width)]
    share = tokens * seq // heads
    others = max(seq // 2 - 1, 1)
    vmem = pl.BlockSpec(memory_space=pltpu.VMEM)
    dma = pltpu.SemaphoreType.DMA
    return pl.pallas_call(
        functools.partial(project_kernel, heads, seq, tile, spans),
        out_shape=jax.ShapeDtypeStruct((share, width), jnp.bfloat16),
        in_specs=[vmem, pl.BlockSpec(memory_space=pl.ANY)],
        out_specs=vmem,
        scratch_shapes=[
            pltpu.VMEM((depth, width), jnp.bfloat16),
            pltpu.VMEM((seq, tokens, depth), jnp.bfloat16),
            pltpu.VMEM((seq * tokens, width), jnp.float32),
            pltpu.VMEM((heads, share, width), jnp.bfloat16),
            pltpu.VMEM((heads, share, width), jnp.bfloat16),
            pltpu.VMEM((heads, share, width), jnp.bfloat16),
            dma((width // tile,)),
            dma((others, PIECES)),
            dma((others, PIECES)),
            dma((seq // 2, PIECES)),
            dma((seq // 2, PIECES)),
            dma((heads, len(spans))),
            dma((heads, len(spans))),
            dma((heads, len(spans))),
        ],
        compiler_params=pltpu.CompilerParams(
            collective_id=1, has_side_effects=True, vmem_limit_bytes=56 * 1024 * 1024
        ),
    )(head_out, out_proj)


def per_device(
    prompt_states,
    new_states,
    prompt_lengths,
    routing,
    row_request,
    queries,
    gain_kv,
    down_kv,
    absorb_k,
    absorb_v,
    out_proj,
):
    owners = lax.axis_size("seq")
    own_index = lax.axis_index("seq")
    requests = prompt_lengths.shape[1]
    per_peer = requests // owners
    pr_rows = prompt_states.shape[0]
    dec_rows = new_states.shape[0]
    heads = lax.axis_size("heads")
    head_index = lax.axis_index("heads")
    cp = pr_rows // heads
    pn = 16 * -(-dec_rows // (16 * heads))
    padded = pn * heads - dec_rows
    request_ids = jnp.arange(requests, dtype=jnp.int32)
    starts_all = jnp.sum(
        jnp.where(
            request_ids[None, None, :] < request_ids[None, :, None],
            prompt_lengths[:, None, :],
            0,
        ),
        axis=2,
    )
    my_starts = lax.dynamic_slice_in_dim(starts_all, own_index, 1)
    row_ids = head_index * cp + jnp.arange(cp, dtype=jnp.int32)
    row_start = jnp.max(
        jnp.where(my_starts <= row_ids[:, None], my_starts, 0), axis=1
    )
    prompt_pos = row_ids - row_start
    source = request_ids // per_peer
    slot_req = lax.dynamic_slice_in_dim(
        routing.reshape(owners, owners, per_peer), own_index, 1, axis=1
    ).reshape(requests)
    chosen = slot_req[:, None] == request_ids[None, :]
    slot_len = jnp.sum(
        jnp.where(chosen, jnp.repeat(prompt_lengths, per_peer, axis=0), 0), axis=1
    )
    slot_first = source * pr_rows + jnp.sum(
        jnp.where(chosen, jnp.repeat(starts_all, per_peer, axis=0), 0), axis=1
    )
    token_ids = jnp.arange(dec_rows, dtype=jnp.int32)
    same_slot = row_request[:, None] == row_request[None, :]
    earlier = jnp.sum(
        (same_slot & (token_ids[:, None] > token_ids[None, :])).astype(jnp.int32), axis=1
    )
    row_slot = row_request[:, None] == request_ids[None, :]
    row_len = jnp.sum(jnp.where(row_slot, slot_len[None, :], 0), axis=1)
    row_first = jnp.sum(jnp.where(row_slot, slot_first[None, :], 0), axis=1)
    new_pos = row_len + earlier
    my_pos = jnp.concatenate(
        [
            prompt_pos,
            lax.dynamic_slice_in_dim(jnp.pad(new_pos, (0, padded)), head_index * pn, pn),
        ]
    )
    cosine, sine = rotation_tables(my_pos)
    prompt_lat, new_lat = latent_rows(
        prompt_states, jnp.pad(new_states, ((0, padded), (0, 0))), down_kv, gain_kv, cosine, sine
    )
    new_lat = new_lat[:dec_rows]
    prompt_lat = prompt_lat.reshape(owners * pr_rows, -1)
    query_latent = jnp.einsum(
        "thn,hnc->thc", queries[:, :, :NOPE], absorb_k, preferred_element_type=jnp.float32
    ).astype(jnp.bfloat16)
    start = jnp.minimum(row_first // 16 * 16, owners * pr_rows - (MAXLEN + 16))
    bias = jnp.where(
        same_slot & (token_ids[None, :] <= token_ids[:, None]), jnp.float32(0), -jnp.inf
    )
    local_heads = queries.shape[1]
    latent_out = attend(
        start,
        row_first - start,
        row_len,
        query_latent.reshape(dec_rows * local_heads, KVL),
        queries[:, :, NOPE:].reshape(dec_rows * local_heads, ROPE),
        bias,
        prompt_lat,
        new_lat,
    ).reshape(dec_rows, local_heads, KVL)
    head_out = jnp.einsum(
        "thc,hcv->thv", latent_out, absorb_v, preferred_element_type=jnp.float32
    ).astype(jnp.bfloat16)
    head_out = head_out.reshape(dec_rows, -1)
    return project(head_out, out_proj)


def solution(mesh):
    return jax.shard_map(
        per_device,
        mesh=mesh,
        in_specs=(
            P(("groups", "seq"), "heads"),
            P(("groups", "seq"), "heads"),
            P("groups", None),
            P("groups", None),
            P(("groups", "seq")),
            P(("groups", "seq"), "heads", None),
            P(),
            P("heads", None),
            P("heads", None, None),
            P("heads", None, None),
            P("heads", "seq"),
        ),
        out_specs=P(("groups", "heads"), "seq"),
        check_vma=False,
    )
```
